128 devices in a mesh: row: 8 (over y, core), col: 16 (over x, z).
Axes of the slice: x: 4, y: 4, z: 4, core: 2. Of those that a mesh axis runs over, the one named last changes fastest.
Arguments:
- queries: bfloat16 [16, 16, 128, 1408], P('row', 'col'), may hold values from -240 to 240
- keys: bfloat16 [16, 16, 128, 1408], P('row', 'col'), may hold values from -6.5 to 6.5
- values: bfloat16 [16, 16, 128, 1408], P('row', 'col'), may hold values from -6 to 6
- dout: bfloat16 [16, 16, 128, 1408], P('row', 'col'), may hold values from -36 to 36
- link_query: int32 [8, 16, 16], replicated, may hold values from 0 to 1
- link_key: int32 [8, 16, 16], replicated, may hold values from 0 to 1
Outputs:
- grad_queries: bfloat16 [16, 16, 128, 1408], P('row', 'col')
- grad_keys: bfloat16 [16, 16, 128, 1408], P('row', 'col')
- grad_values: bfloat16 [16, 16, 128, 1408], P('row', 'col')
The draws below stay inside these ranges and needn't reach their ends.
All inputs are finite; a program needn't handle non-finite values.
Results may differ from the reference program's by a relative error of at most 0.015.
Values may be sent and summed in bfloat16 or wider, within the bound.
A program may use at most 256 MiB of HBM per device.

```python
import jax
import jax.numpy as jnp
from jax import lax

D = 1408
HEADS = 16
BLK = 128
PR = 2
PC = 1
GR = 16
GC = 16
N_ROW = 8
N_COL = 16


def shared_keys(key):
    return jnp.clip(jax.random.normal(key, (GR, GC, BLK, D), jnp.float32), -6.0, 6.0)


def draw_queries(key, part):
    key = jax.random.fold_in(key, 7)
    first = jax.random.fold_in(key, 0)
    return jnp.clip(jax.random.normal(first, (GR, GC, BLK, D), jnp.float32), -6.0, 6.0).astype(jnp.bfloat16)


def draw_keys(key, part):
    base = shared_keys(key)
    return base.astype(jnp.bfloat16)


def plant(result, own_key, least, top_value):
    place = [jax.random.randint(jax.random.fold_in(own_key, axis), (), 0, length) for axis, length in enumerate(result.shape)]
    longest = result.shape.index(max(result.shape))
    next_to = place[:longest] + [(place[longest] + 1) % result.shape[longest]] + place[longest + 1:]
    return result.at[tuple(place)].set(least).at[tuple(next_to)].set(top_value)


def shard_levels(own_key, extent, cuts, low, largest):
    def one(position, parts):
        heights = jax.random.uniform(jax.random.fold_in(jax.random.fold_in(own_key, 6), position), (parts,), jnp.float32, low / len(cuts), largest / len(cuts))
        return jnp.repeat(jnp.exp(heights), extent[position] // parts).reshape((-1,) + (1,) * (len(extent) - position - 1))

    factor_of = one(*cuts[0])
    for cut in cuts[1:]:
        factor_of = factor_of * one(*cut)
    return factor_of


def gaussian(own_key, extent, deviation, limit, cuts=(), kind=jnp.bfloat16):
    values = jax.random.normal(own_key, extent, jnp.float32) * deviation
    if len(cuts) > 0:
        values = shard_levels(own_key, extent, cuts, -0.22, 0.18) * values
    return jnp.clip(values, min=-limit, max=limit).astype(kind)


def setup_inputs(seed: int = 0) -> dict:
    key_list = jax.random.split(jax.random.key(seed), 7)
    queries = draw_queries(jax.random.fold_in(key_list[6], 71), 0)
    keys = draw_keys(jax.random.fold_in(key_list[6], 71), 0)
    values = gaussian(key_list[2], (GR, GC, BLK, D), 1.0, 6.0, ((0, 8), (1, 16)))
    dout = gaussian(key_list[3], (GR, GC, BLK, D), 6.0, 36.0, ((0, 8), (1, 16)))
    link_query = plant(jax.random.randint(key_list[4], (N_ROW, N_COL, N_COL), 0, PR * PC), jax.random.fold_in(key_list[4], 1), 0, (PR * PC) - 1).astype(jnp.int32)
    link_key = plant(jax.random.randint(key_list[5], (N_ROW, N_COL, N_COL), 0, PR * PC), jax.random.fold_in(key_list[5], 1), 0, (PR * PC) - 1).astype(jnp.int32)
    return dict(queries=queries, keys=keys, values=values, dout=dout, link_query=link_query, link_key=link_key)


window_rows = (0, -1, 1, 0, 0)
window_cols = (0, 0, 0, -1, 1)
highest = lax.Precision.HIGHEST


def round_keep(source_value):
    return lax.optimization_barrier(source_value.astype(jnp.bfloat16)).astype(jnp.float32)


def with_heads(source_array):
    return source_array.astype(jnp.float32).reshape(source_array.shape[:-1] + (HEADS, D // HEADS))


def merge_heads(source_array):
    return source_array.reshape(source_array.shape[:-2] + (D,))


def reference(queries, keys, values, dout, link_query, link_key):
    score_scale = (D // HEADS) ** -0.5
    block_count = PR * PC
    local_ids = jnp.arange(block_count, dtype=jnp.int32)
    step_rows = jnp.array(window_rows, jnp.int32)
    step_cols = jnp.array(window_cols, jnp.int32)

    def device_step(state_grads, device):
        query_total, key_total, value_total = state_grads
        row_index = device // N_COL
        col_index = device % N_COL
        query_rows = row_index * PR + local_ids // PC
        query_cols = col_index * PC + local_ids % PC
        near_rows = query_rows[:, None] + step_rows[None, :]
        near_cols = query_cols[:, None] + step_cols[None, :]
        inside = (near_rows >= 0) & (near_rows < GR) & (near_cols >= 0) & (near_cols < GC)
        zero_column = jnp.zeros((block_count, 1), jnp.int32)
        slot_rows = jnp.concatenate([jnp.clip(near_rows, 0, GR - 1), zero_column], 1)
        slot_cols = jnp.concatenate([jnp.clip(near_cols, 0, GC - 1), zero_column], 1)
        usable = jnp.concatenate([inside, jnp.ones((block_count, 1), jnp.bool_)], 1)
        other_patch = (slot_rows // PR != row_index) | (slot_cols // PC != col_index)
        is_window = (jnp.arange(6) < 5)[None, :]
        to_round = usable & other_patch & is_window
        query_pick = link_query[row_index, col_index]
        key_pick = link_key[row_index, col_index]
        rand_rows = row_index * PR + key_pick // PC
        rand_cols = jnp.arange(N_COL, dtype=jnp.int32) * PC + key_pick % PC
        query_onehot = (query_pick[:, None] == local_ids[None, :]).astype(jnp.float32)

        query_group = with_heads(queries[query_rows, query_cols])
        grad_out = with_heads(dout[query_rows, query_cols])
        keys_window = with_heads(keys[slot_rows, slot_cols])
        values_window = with_heads(values[slot_rows, slot_cols])
        keys_random = with_heads(keys[rand_rows, rand_cols])
        values_random = with_heads(values[rand_rows, rand_cols])
        query_random = query_group[query_pick]
        dout_random = grad_out[query_pick]

        scores_window = jnp.einsum('bqhd,bskhd->bhqsk', query_group, keys_window) * score_scale
        scores_window = jnp.where(usable[:, None, None, :, None], scores_window, -jnp.inf)
        scores_random = jnp.einsum('rqhd,rkhd->rhqk', query_random, keys_random) * score_scale
        top_random = jnp.max(scores_random, axis=3)
        peak_score = jnp.maximum(
            jnp.max(scores_window, axis=(3, 4)),
            jnp.max(jnp.where(query_onehot[:, :, None, None] > 0, top_random[:, None], -jnp.inf), axis=0))
        peak_slot = peak_score[query_pick]
        normalizer = jnp.sum(jnp.exp(scores_window - peak_score[..., None, None]), axis=(3, 4))
        normalizer = normalizer + jnp.einsum(
            'rb,rhq->bhq', query_onehot, jnp.sum(jnp.exp(scores_random - peak_slot[..., None]), axis=3), precision=highest)
        log_total = peak_score + jnp.log(normalizer)
        log_slot = log_total[query_pick]

        weights_window = jnp.exp(scores_window - log_total[..., None, None])
        weights_random = jnp.exp(scores_random - log_slot[..., None])
        rounded_window = round_keep(weights_window)
        rounded_random = round_keep(weights_random)
        attended = jnp.einsum('bhqsk,bskhd->bqhd', rounded_window, values_window)
        attended = attended + jnp.einsum(
            'rb,rqhd->bqhd', query_onehot, jnp.einsum('rhqk,rkhd->rqhd', rounded_random, values_random), precision=highest)
        row_delta = jnp.moveaxis(jnp.sum(grad_out * attended, axis=3), 1, 2)
        delta_slot = row_delta[query_pick]

        upstream_window = jnp.einsum('bqhd,bskhd->bhqsk', grad_out, values_window)
        slopes_window = round_keep(score_scale * weights_window * (upstream_window - row_delta[..., None, None]))
        upstream_random = jnp.einsum('rqhd,rkhd->rhqk', dout_random, values_random)
        slopes_random = round_keep(score_scale * weights_random * (upstream_random - delta_slot[..., None]))

        query_grad = jnp.einsum('bhqsk,bskhd->bqhd', slopes_window, keys_window)
        query_grad = query_grad + jnp.einsum(
            'rb,rqhd->bqhd', query_onehot, jnp.einsum('rhqk,rkhd->rqhd', slopes_random, keys_random), precision=highest)
        key_window = merge_heads(jnp.einsum('bhqsk,bqhd->bskhd', slopes_window, query_group))
        value_window = merge_heads(jnp.einsum('bhqsk,bqhd->bskhd', rounded_window, grad_out))
        key_random = round_keep(merge_heads(jnp.einsum('rhqk,rqhd->rkhd', slopes_random, query_random)))
        value_random = round_keep(merge_heads(jnp.einsum('rhqk,rqhd->rkhd', rounded_random, dout_random)))
        round_mask = to_round[:, :, None, None]
        key_window = jnp.where(round_mask, round_keep(key_window), key_window)
        value_window = jnp.where(round_mask, round_keep(value_window), value_window)

        query_total = query_total.at[query_rows, query_cols].set(merge_heads(query_grad))
        key_total = key_total.at[slot_rows, slot_cols].add(key_window).at[rand_rows, rand_cols].add(key_random)
        value_total = value_total.at[slot_rows, slot_cols].add(value_window).at[rand_rows, rand_cols].add(value_random)
        return (query_total, key_total, value_total), None

    empty_grid = jnp.zeros((GR, GC, BLK, D), jnp.float32)
    devices = jnp.arange(N_ROW * N_COL, dtype=jnp.int32)
    (query_total, key_total, value_total), _ = lax.scan(device_step, (empty_grid, empty_grid, empty_grid), devices)
    return (query_total.astype(jnp.bfloat16), key_total.astype(jnp.bfloat16), value_total.astype(jnp.bfloat16))
```

```python
import functools

import jax
import jax.numpy as jnp
from jax import lax
from jax.experimental import pallas as pl
from jax.experimental.pallas import tpu as pltpu
from jax.sharding import PartitionSpec as P

D = 1408
HEADS = 16
HD = D // HEADS
BLK = 128
ROWS = 8
COLS = 16
SIDE = 4
PAIR = 2 * HD
TILES = D // BLK
ABOVE = 2 * COLS
BELOW = 3 * COLS
GLOBAL = 4 * COLS
KEY_BLOCKS = GLOBAL + 1
WINDOW = 12
SLOTS = WINDOW + COLS
SCALE = HD ** (-0.5)
LOG2E = 1.4426950408889634
NEG = -1e30
MESH = pl.DeviceIdType.MESH
f32 = jnp.float32
bf16 = jnp.bfloat16


def moved(col, step):
    x = lax.rem(col // SIDE + step // SIDE + SIDE, SIDE)
    z = lax.rem(lax.rem(col, SIDE) + lax.rem(step, SIDE) + SIDE, SIDE)
    return x * SIDE + z


def moved_back(col, step):
    x = lax.rem(col // SIDE - step // SIDE + SIDE, SIDE)
    z = lax.rem(lax.rem(col, SIDE) - lax.rem(step, SIDE) + SIDE, SIDE)
    return x * SIDE + z


def loop(low, high, body):
    def step(i, carry):
        body(i)
        return carry

    lax.fori_loop(low, high, step, 0)


def greet(row, col):
    barrier = pltpu.get_barrier_semaphore()

    def signal_col(step):
        pl.semaphore_signal(barrier, inc=1, device_id=(row, moved(col, step)), device_id_type=MESH)

    def signal_row(step):
        pl.semaphore_signal(barrier, inc=1, device_id=(lax.rem(row + step, ROWS), col), device_id_type=MESH)

    loop(1, COLS, signal_col)
    loop(1, ROWS, signal_row)


def meet():
    pl.semaphore_wait(pltpu.get_barrier_semaphore(), COLS - 1 + ROWS - 1)


def scatter_heads(
    q_ref, k_ref, v_ref, o_ref, keys_out, query_out,
    xt_a, xt_b, send_kv, send_qo, own_sem, send_sem, recv_sem, halo_send, halo_recv, globe_send, globe_recv,
):
    row = lax.axis_index("row")
    col = lax.axis_index("col")
    up = lax.rem(row + ROWS - 1, ROWS)
    down = lax.rem(row + 1, ROWS)
    greet(row, col)

    def pack(first, second, buffer):
        def pack_block(i):
            for source, turned in ((first, xt_a), (second, xt_b)):
                for t in range(TILES):
                    span = slice(t * BLK, (t + 1) * BLK)
                    turned[span, :] = source[i, :, span].astype(f32).T
            for h in range(HEADS):
                span = slice(h * HD, (h + 1) * HD)
                buffer[h, i] = jnp.concatenate([xt_a[span, :], xt_b[span, :]], 0).astype(bf16)

        loop(0, 2, pack_block)

    def outgoing(kind, buffer, out, step):
        dest = moved(col, step)
        return pltpu.make_async_remote_copy(
            src_ref=buffer.at[dest],
            dst_ref=out.at[pl.ds(2 * col, 2)],
            send_sem=send_sem.at[kind, step],
            recv_sem=recv_sem.at[kind, step],
            device_id=(row, dest),
            device_id_type=MESH,
        )

    def incoming(kind, buffer, out, step):
        source = moved_back(col, step)
        return pltpu.make_async_remote_copy(
            src_ref=buffer.at[source],
            dst_ref=out.at[pl.ds(2 * source, 2)],
            send_sem=send_sem.at[kind, step],
            recv_sem=recv_sem.at[kind, step],
            device_id=(row, source),
            device_id_type=MESH,
        )

    def halo(way, source):
        return pltpu.make_async_remote_copy(
            src_ref=keys_out.at[2 * source + way],
            dst_ref=keys_out.at[(BELOW if way == 0 else ABOVE) + source],
            send_sem=halo_send.at[way, source],
            recv_sem=halo_recv.at[way, source],
            device_id=(up if way == 0 else down, col),
            device_id_type=MESH,
        )

    def globe(target):
        return pltpu.make_async_remote_copy(
            src_ref=keys_out.at[0],
            dst_ref=keys_out.at[GLOBAL],
            send_sem=globe_send.at[target],
            recv_sem=globe_recv.at[0],
            device_id=(target, col),
            device_id_type=MESH,
        )

    pack(k_ref, v_ref, send_kv)
    meet()
    loop(1, COLS, lambda step: outgoing(0, send_kv, keys_out, step).start())
    own_kv = pltpu.make_async_copy(send_kv.at[col], keys_out.at[pl.ds(2 * col, 2)], own_sem.at[0])
    own_kv.start()
    pack(q_ref, o_ref, send_qo)
    loop(1, COLS, lambda step: outgoing(1, send_qo, query_out, step).start())
    own_qo = pltpu.make_async_copy(send_qo.at[col], query_out.at[pl.ds(2 * col, 2)], own_sem.at[1])
    own_qo.start()
    own_kv.wait()

    def pass_on(source):
        for way in range(2):
            halo(way, source).start()

    pass_on(col)

    def landed(step):
        incoming(0, send_kv, keys_out, step).wait_recv()
        pass_on(moved_back(col, step))

    loop(1, COLS, landed)

    @pl.when(row == 0)
    def _():
        loop(1, ROWS, lambda target: globe(target).start())
        own_globe = pltpu.make_async_copy(keys_out.at[0], keys_out.at[GLOBAL], own_sem.at[2])
        own_globe.start()
        own_globe.wait()

    own_qo.wait()
    loop(1, COLS, lambda step: incoming(1, send_qo, query_out, step).wait_recv())
    loop(0, COLS, lambda source: [halo(way, source).wait_recv() for way in range(2)])

    @pl.when(row != 0)
    def _():
        globe(0).wait_recv()

    loop(1, COLS, lambda step: outgoing(0, send_kv, keys_out, step).wait_send())
    loop(1, COLS, lambda step: outgoing(1, send_qo, query_out, step).wait_send())
    loop(0, COLS, lambda source: [halo(way, source).wait_send() for way in range(2)])

    @pl.when(row == 0)
    def _():
        loop(1, ROWS, lambda target: globe(target).wait_send())


def attend(
    link_query, link_key, keys_ref, query_ref, dq_out, own_out, halo_out, globe_out,
    kvn, acc, both, both_t, p_s, u_s, m_s, l_s, a_s, f_s, delta_s, dq_s,
):
    row = lax.axis_index("row")
    factor = SCALE * LOG2E
    top_rows = lax.broadcasted_iota(jnp.int32, (PAIR, BLK), 0) < HD
    left_lanes = lax.broadcasted_iota(jnp.int32, (BLK, PAIR), 1) < HD
    scale_rows = jnp.where(top_rows, f32(SCALE), f32(1.0))

    def prepare(b):
        kvn[b] = keys_ref[b].astype(f32).T.astype(bf16)
        acc[b] = jnp.zeros((BLK, PAIR), f32)

    loop(0, KEY_BLOCKS, prepare)

    def forward(i, block, t, usable):
        su = jnp.dot(kvn[block], both[i], preferred_element_type=f32)
        s, u = su[:, :BLK], su[:, BLK:]
        m = jnp.max(s, axis=0, keepdims=True)
        p = jnp.exp2((s - m) * factor)
        p_s[t] = p
        u_s[t] = u
        m_s[i, pl.ds(t, 1), :] = m if usable is None else jnp.where(usable, m, NEG)
        l_s[i, pl.ds(t, 1), :] = jnp.sum(p, axis=0, keepdims=True)
        a_s[i, pl.ds(t, 1), :] = jnp.sum(p * u, axis=0, keepdims=True)

    def backward(i, block, t):
        w = p_s[t] * f_s[i, pl.ds(t, 1), :]
        slope = w * (u_s[t] - delta_s[i])
        slope_b = slope.astype(bf16)
        terms = jnp.concatenate([slope_b, w.astype(bf16)], 1)
        acc[block] += jnp.dot(terms, both_t[i], preferred_element_type=f32)
        return jnp.dot(keys_ref[block, :HD, :], slope_b, preferred_element_type=f32)

    def patch(c):
        left = jnp.maximum(c - 1, 0)
        right = jnp.minimum(c + 1, COLS - 1)
        window = []
        for i in range(2):
            window.append((i, 2 * c + i, None))
            window.append((i, 2 * c + 1 - i, None))
            window.append((i, (ABOVE if i == 0 else BELOW) + c, (row > 0) if i == 0 else (row < ROWS - 1)))
            window.append((i, 2 * left + i, c > 0))
            window.append((i, 2 * right + i, c < COLS - 1))
            window.append((i, GLOBAL, None))
        for i in range(2):
            pair = query_ref[2 * c + i]
            zero = jnp.zeros_like(pair)
            both[i] = jnp.concatenate([jnp.where(top_rows, pair, zero), jnp.where(top_rows, zero, pair)], 1)
            turned = pair.astype(f32).T
            none = jnp.zeros_like(turned)
            both_t[i] = jnp.concatenate(
                [jnp.where(left_lanes, turned, none), jnp.where(left_lanes, none, turned)], 0
            ).astype(bf16)
        m_s[...] = jnp.full(m_s.shape, NEG, f32)
        l_s[...] = jnp.zeros(l_s.shape, f32)
        a_s[...] = jnp.zeros(a_s.shape, f32)

        for t, (i, block, usable) in enumerate(window):
            forward(i, block, t, usable)

        def link(q):
            return link_query[row, c, q], 2 * q + link_key[row, c, q]

        def forward_links(g):
            for e in range(4):
                q = 4 * g + e
                i, block = link(q)
                forward(i, block, WINDOW + q, None)

        loop(0, COLS // 4, forward_links)

        for i in range(2):
            peak = m_s[i]
            top = jnp.max(peak, axis=0, keepdims=True)
            part = jnp.exp2((peak - top) * factor)
            inverse = 1.0 / jnp.sum(l_s[i] * part, axis=0, keepdims=True)
            delta_s[i] = jnp.sum(a_s[i] * part, axis=0, keepdims=True) * inverse
            f_s[i] = part * inverse

        for i in range(2):
            total = None
            for t, (own, block, _) in enumerate(window):
                if own == i:
                    term = backward(i, block, t)
                    total = term if total is None else total + term
            dq_s[i] = total

        def backward_links(g):
            for e in range(4):
                q = 4 * g + e
                i, block = link(q)
                dq_s[i] += backward(i, block, WINDOW + q)

        loop(0, COLS // 4, backward_links)
        dq_out[c] = (jnp.concatenate([dq_s[0], dq_s[1]], 0) * SCALE).astype(bf16)

    loop(0, COLS, patch)

    def finish_own(b):
        own_out[b] = acc[b].T * scale_rows

    def finish_halo(b):
        halo_out[b] = (acc[ABOVE + b].T * scale_rows).astype(bf16)

    loop(0, ABOVE, finish_own)
    loop(0, ABOVE, finish_halo)
    globe_out[...] = acc[GLOBAL].T * scale_rows


def gather_heads(
    dq_ref, own_ref, halo_ref, globe_ref, gq_out, gk_out, gv_out,
    got_dq, send_kv, got_kv, halo_in, globe_in, globe_sum, wide,
    own_sem, send_sem, recv_sem, halo_send, halo_recv, globe_send, globe_recv,
):
    row = lax.axis_index("row")
    col = lax.axis_index("col")
    up = lax.rem(row + ROWS - 1, ROWS)
    down = lax.rem(row + 1, ROWS)
    greet(row, col)

    def outgoing(kind, buffer, slots, step):
        dest = moved(col, step)
        return pltpu.make_async_remote_copy(
            src_ref=buffer.at[dest],
            dst_ref=slots.at[col],
            send_sem=send_sem.at[kind, step],
            recv_sem=recv_sem.at[kind, step],
            device_id=(row, dest),
            device_id_type=MESH,
        )

    def incoming(kind, buffer, slots, step):
        source = moved_back(col, step)
        return pltpu.make_async_remote_copy(
            src_ref=buffer.at[source],
            dst_ref=slots.at[source],
            send_sem=send_sem.at[kind, step],
            recv_sem=recv_sem.at[kind, step],
            device_id=(row, source),
            device_id_type=MESH,
        )

    def halo(way, c):
        return pltpu.make_async_remote_copy(
            src_ref=halo_ref.at[way * COLS + c],
            dst_ref=halo_in.at[1 - way, c],
            send_sem=halo_send.at[way, c],
            recv_sem=halo_recv.at[way, c],
            device_id=(up if way == 0 else down, col),
            device_id_type=MESH,
        )

    def globe(slot):
        return pltpu.make_async_remote_copy(
            src_ref=globe_ref,
            dst_ref=globe_in.at[slot],
            send_sem=globe_send.at[0],
            recv_sem=globe_recv.at[slot],
            device_id=(0, col),
            device_id_type=MESH,
        )

    meet()
    globe_sum[...] = jnp.zeros(globe_sum.shape, f32)

    @pl.when(row != 0)
    def _():
        globe(row).start()

    def start_halo(step):
        c = moved(col, step)
        for way in range(2):
            halo(way, c).start()

    loop(0, COLS, start_halo)
    loop(1, COLS, lambda step: outgoing(0, dq_ref, got_dq, step).start())
    own_dq = pltpu.make_async_copy(dq_ref.at[col], got_dq.at[col], own_sem.at[0])
    own_dq.start()

    @pl.when(row == 0)
    def _():
        loop(1, ROWS, lambda slot: globe(slot).wait_recv())
        total = globe_ref[...]
        for slot in range(1, ROWS):
            total = total + globe_in[slot]
        globe_sum[...] = total

    def combine(c):
        for way in range(2):
            halo(1 - way, c).wait_recv()
        for i in range(2):
            total = own_ref[2 * c + i] + halo_in[i, c].astype(f32)
            if i == 0:
                total = total + jnp.where(c == 0, globe_sum[...], 0.0)
            send_kv[c, i] = total.astype(bf16)

    def combine_and_send(step):
        combine(moved(col, step))
        outgoing(1, send_kv, got_kv, step).start()

    loop(1, COLS, combine_and_send)
    combine(col)
    own_kv = pltpu.make_async_copy(send_kv.at[col], got_kv.at[col], own_sem.at[1])
    own_kv.start()

    def unpack(i, load, out):
        for h in range(HEADS):
            wide[h * HD : (h + 1) * HD, :] = load(h)
        for t in range(TILES):
            span = slice(t * BLK, (t + 1) * BLK)
            out[i, :, span] = wide[span, :].T.astype(bf16)

    own_dq.wait()
    loop(1, COLS, lambda step: incoming(0, dq_ref, got_dq, step).wait_recv())
    for i in range(2):
        unpack(i, lambda h: got_dq[h].astype(f32)[i * HD : (i + 1) * HD], gq_out)
    own_kv.wait()
    loop(1, COLS, lambda step: incoming(1, send_kv, got_kv, step).wait_recv())

    def unpack_kv(i):
        unpack(i, lambda h: got_kv[h, i].astype(f32)[:HD], gk_out)
        unpack(i, lambda h: got_kv[h, i].astype(f32)[HD:], gv_out)

    loop(0, 2, unpack_kv)

    loop(1, COLS, lambda step: outgoing(0, dq_ref, got_dq, step).wait_send())
    loop(1, COLS, lambda step: outgoing(1, send_kv, got_kv, step).wait_send())
    loop(0, COLS, lambda c: [halo(way, c).wait_send() for way in range(2)])

    @pl.when(row != 0)
    def _():
        globe(row).wait_send()


VMEM = pl.BlockSpec(memory_space=pltpu.VMEM)
ANY = pl.BlockSpec(memory_space=pl.ANY)
SMEM = pl.BlockSpec(memory_space=pltpu.SMEM)
DMA = pltpu.SemaphoreType.DMA
LIMIT = 58 * 1024 * 1024


def shape(dims, kind):
    return jax.ShapeDtypeStruct(dims, kind)


def shards(queries, keys, values, dout, link_query, link_key):
    flat = [a.reshape(2, BLK, D) for a in (queries, keys, values, dout)]
    packed_kv, packed_q = pl.pallas_call(
        scatter_heads,
        out_shape=(shape((KEY_BLOCKS, PAIR, BLK), bf16), shape((2 * COLS, PAIR, BLK), bf16)),
        in_specs=[VMEM] * 4,
        out_specs=(ANY, ANY),
        scratch_shapes=[
            pltpu.VMEM((D, BLK), f32),
            pltpu.VMEM((D, BLK), f32),
            pltpu.VMEM((HEADS, 2, PAIR, BLK), bf16),
            pltpu.VMEM((HEADS, 2, PAIR, BLK), bf16),
            DMA((3,)),
            DMA((2, COLS)),
            DMA((2, COLS)),
            DMA((2, COLS)),
            DMA((2, COLS)),
            DMA((ROWS,)),
            DMA((1,)),
        ],
        compiler_params=pltpu.CompilerParams(collective_id=0, has_side_effects=True, vmem_limit_bytes=LIMIT),
        name="scatter_heads",
    )(*flat)
    dq, own, halo, globe = pl.pallas_call(
        attend,
        out_shape=(
            shape((COLS, PAIR, BLK), bf16),
            shape((2 * COLS, PAIR, BLK), f32),
            shape((2 * COLS, PAIR, BLK), bf16),
            shape((PAIR, BLK), f32),
        ),
        in_specs=[SMEM, SMEM, VMEM, VMEM],
        out_specs=(VMEM,) * 4,
        scratch_shapes=[
            pltpu.VMEM((KEY_BLOCKS, BLK, PAIR), bf16),
            pltpu.VMEM((KEY_BLOCKS, BLK, PAIR), f32),
            pltpu.VMEM((2, PAIR, 2 * BLK), bf16),
            pltpu.VMEM((2, 2 * BLK, PAIR), bf16),
            pltpu.VMEM((SLOTS, BLK, BLK), f32),
            pltpu.VMEM((SLOTS, BLK, BLK), f32),
            pltpu.VMEM((2, 32, BLK), f32),
            pltpu.VMEM((2, 32, BLK), f32),
            pltpu.VMEM((2, 32, BLK), f32),
            pltpu.VMEM((2, 32, BLK), f32),
            pltpu.VMEM((2, 1, BLK), f32),
            pltpu.VMEM((2, HD, BLK), f32),
        ],
        compiler_params=pltpu.CompilerParams(vmem_limit_bytes=LIMIT),
        name="attend",
    )(link_query, link_key, packed_kv, packed_q)
    outs = pl.pallas_call(
        gather_heads,
        out_shape=(shape((2, BLK, D), bf16),) * 3,
        in_specs=[VMEM] * 4,
        out_specs=(VMEM,) * 3,
        scratch_shapes=[
            pltpu.VMEM((COLS, PAIR, BLK), bf16),
            pltpu.VMEM((COLS, 2, PAIR, BLK), bf16),
            pltpu.VMEM((COLS, 2, PAIR, BLK), bf16),
            pltpu.VMEM((2, COLS, PAIR, BLK), bf16),
            pltpu.VMEM((ROWS, PAIR, BLK), f32),
            pltpu.VMEM((PAIR, BLK), f32),
            pltpu.VMEM((D, BLK), f32),
            DMA((2,)),
            DMA((2, COLS)),
            DMA((2, COLS)),
            DMA((2, COLS)),
            DMA((2, COLS)),
            DMA((1,)),
            DMA((ROWS,)),
        ],
        compiler_params=pltpu.CompilerParams(collective_id=1, has_side_effects=True, vmem_limit_bytes=LIMIT),
        name="gather_heads",
    )(dq, own, halo, globe)
    return tuple(o.reshape(2, 1, BLK, D) for o in outs)


def solution(mesh):
    tiled = P("row", "col", None, None)
    return jax.shard_map(
        shards,
        mesh=mesh,
        in_specs=(tiled,) * 4 + (P(), P()),
        out_specs=(tiled,) * 3,
        check_vma=False,
    )
```

```python
import jax
import jax.numpy as jnp
from jax import lax
from jax.experimental import pallas as pl
from jax.experimental.pallas import tpu as pltpu
from jax.sharding import PartitionSpec as P

D = 1408
HEADS = 16
HD = D // HEADS
BLK = 128
ROWS = 8
COLS = 16
SIDE = 4
STRIDE = 5
PAIR = 2 * HD
TILES = D // BLK
ABOVE = 2 * COLS
BELOW = 3 * COLS
GLOBAL = 4 * COLS
KEY_BLOCKS = GLOBAL + 1
WINDOW = 12
SLOTS = WINDOW + COLS
SCALE = HD ** (-0.5)
LOG2E = 1.4426950408889634
NEG = -1e30
MESH = pl.DeviceIdType.MESH
f32 = jnp.float32
bf16 = jnp.bfloat16


def shifted(row, col, step, sign):
    core = lax.rem(row, 2)
    turn = lax.rem(step * STRIDE, COLS)
    first, second = turn // SIDE, lax.rem(turn, SIDE)
    dx = sign * (first * (1 - core) + (SIDE - second) * core)
    dz = sign * (second * (1 - core) + (SIDE - first) * core)
    x = lax.rem(col // SIDE + dx + SIDE, SIDE)
    z = lax.rem(lax.rem(col, SIDE) + dz + SIDE, SIDE)
    return x * SIDE + z


def loop(low, high, body):
    def step(i, carry):
        body(i)
        return carry

    lax.fori_loop(low, high, step, 0)


def turned_dot(a, b):
    return lax.dot_general(a, b, (((1,), (1,)), ((), ())), preferred_element_type=f32)


def attend(
    link_query, link_key, q_ref, k_ref, v_ref, o_ref, got_dq, got_kv,
    xt_a, xt_b, send_kv, send_qo, keys, query, kvn, both, pairs, p_s, u_s,
    m_s, l_s, a_s, f_s, d_s, i_s, send_dq, send_terms, halo_out, halo_in, globe_acc, globe_in,
    own_sem, send_sem, recv_sem, halo_send, halo_recv, back_send, back_recv, globe_send, globe_recv,
):
    row = lax.axis_index("row")
    col = lax.axis_index("col")
    up = lax.rem(row + ROWS - 1, ROWS)
    down = lax.rem(row + 1, ROWS)
    factor = SCALE * LOG2E

    barrier = pltpu.get_barrier_semaphore()

    def greet(dest_row, dest_col):
        pl.semaphore_signal(barrier, inc=1, device_id=(dest_row, dest_col), device_id_type=MESH)

    loop(1, COLS, lambda step: greet(row, lax.rem(col + step, COLS)))
    loop(1, ROWS, lambda step: greet(lax.rem(row + step, ROWS), col))

    def to_col(kind, source_ref, target_ref, step, sign):
        return pltpu.make_async_remote_copy(
            src_ref=source_ref,
            dst_ref=target_ref,
            send_sem=send_sem.at[kind, step],
            recv_sem=recv_sem.at[kind, step],
            device_id=(row, shifted(row, col, step, sign)),
            device_id_type=MESH,
        )

    def scatter(kind, buffer, out, step):
        return to_col(kind, buffer.at[shifted(row, col, step, 1)], out.at[pl.ds(2 * col, 2)], step, 1)

    def scattered(kind, buffer, out, step):
        source = shifted(row, col, step, -1)
        return to_col(kind, buffer.at[source], out.at[pl.ds(2 * source, 2)], step, -1)

    def gather(kind, buffer, out, step):
        return to_col(kind, buffer.at[shifted(row, col, step, 1)], out.at[col], step, 1)

    def gathered(kind, buffer, out, step):
        source = shifted(row, col, step, -1)
        return to_col(kind, buffer.at[source], out.at[source], step, -1)

    def halo(way, source):
        return pltpu.make_async_remote_copy(
            src_ref=keys.at[2 * source + way],
            dst_ref=keys.at[(BELOW if way == 0 else ABOVE) + source],
            send_sem=halo_send.at[way, source],
            recv_sem=halo_recv.at[way, source],
            device_id=(up if way == 0 else down, col),
            device_id_type=MESH,
        )

    def halo_back(way, c):
        return pltpu.make_async_remote_copy(
            src_ref=halo_out.at[way, c],
            dst_ref=halo_in.at[1 - way, c],
            send_sem=back_send.at[way, c],
            recv_sem=back_recv.at[way, c],
            device_id=(up if way == 0 else down, col),
            device_id_type=MESH,
        )

    def globe(target):
        return pltpu.make_async_remote_copy(
            src_ref=keys.at[0],
            dst_ref=keys.at[GLOBAL],
            send_sem=globe_send.at[target],
            recv_sem=globe_recv.at[0],
            device_id=(target, col),
            device_id_type=MESH,
        )

    def globe_back(slot):
        return pltpu.make_async_remote_copy(
            src_ref=globe_acc,
            dst_ref=globe_in.at[slot],
            send_sem=globe_send.at[0],
            recv_sem=globe_recv.at[slot],
            device_id=(0, col),
            device_id_type=MESH,
        )

    def pack(first, second, buffer):
        def pack_block(i):
            for source, turned in ((first, xt_a), (second, xt_b)):
                for t in range(TILES):
                    span = slice(t * BLK, (t + 1) * BLK)
                    turned[span, :] = source[i, :, span].astype(f32).T
            for h in range(HEADS):
                span = slice(h * HD, (h + 1) * HD)
                buffer[h, i] = jnp.concatenate([xt_a[span, :], xt_b[span, :]], 0).astype(bf16)

        loop(0, 2, pack_block)

    def prepare(b):
        kvn[b] = keys[b].astype(f32).T.astype(bf16)

    pack(k_ref, v_ref, send_kv)
    pl.semaphore_wait(barrier, COLS - 1 + ROWS - 1)
    loop(1, COLS, lambda step: scatter(0, send_kv, keys, step).start())
    own_kv = pltpu.make_async_copy(send_kv.at[col], keys.at[pl.ds(2 * col, 2)], own_sem.at[0])
    own_kv.start()
    pack(q_ref, o_ref, send_qo)
    loop(1, COLS, lambda step: scatter(1, send_qo, query, step).start())
    own_qo = pltpu.make_async_copy(send_qo.at[col], query.at[pl.ds(2 * col, 2)], own_sem.at[1])
    own_qo.start()
    own_kv.wait()

    def pass_on(source):
        for way in range(2):
            halo(way, source).start()
        for way in range(2):
            prepare(2 * source + way)

    pass_on(col)

    def landed(step):
        scattered(0, send_kv, keys, step).wait_recv()
        pass_on(shifted(row, col, step, -1))

    loop(1, COLS, landed)

    @pl.when(row == 0)
    def _():
        loop(1, ROWS, lambda target: globe(target).start())
        own_globe = pltpu.make_async_copy(keys.at[0], keys.at[GLOBAL], own_sem.at[2])
        own_globe.start()
        own_globe.wait()

    def halo_landed(source):
        for way in range(2):
            halo(way, source).wait_recv()
        prepare(ABOVE + source)
        prepare(BELOW + source)

    loop(0, COLS, halo_landed)

    @pl.when(row != 0)
    def _():
        globe(0).wait_recv()

    prepare(GLOBAL)
    own_qo.wait()

    top_rows = lax.broadcasted_iota(jnp.int32, (PAIR, BLK), 0) < HD
    scale_rows = jnp.where(top_rows, f32(SCALE), f32(1.0))
    globe_acc[...] = jnp.zeros(globe_acc.shape, f32)
    m_s[...] = jnp.full(m_s.shape, NEG, f32)
    l_s[...] = jnp.zeros(l_s.shape, f32)
    a_s[...] = jnp.zeros(a_s.shape, f32)
    i_s[...] = jnp.zeros(i_s.shape, f32)
    i_s[6:WINDOW, :] = jnp.ones((6, BLK), f32)
    i_s[SLOTS:, :] = jnp.full((32 - SLOTS, BLK), 2.0, f32)

    def forward(n, block, t, usable):
        su = jnp.dot(kvn[block], both[n], preferred_element_type=f32)
        s, u = su[:, :BLK], su[:, BLK:]
        m = jnp.max(s, axis=0, keepdims=True)
        p = jnp.exp2((s - m) * factor)
        p_s[t] = p
        u_s[t] = u
        m_s[t : t + 1, :] = m if usable is None else jnp.where(usable, m, NEG)
        l_s[t : t + 1, :] = jnp.sum(p, axis=0, keepdims=True)
        a_s[t : t + 1, :] = jnp.sum(p * u, axis=0, keepdims=True)

    def backward(c, block, t):
        w = p_s[t] * f_s[t : t + 1, :]
        slope = w * (u_s[t] - d_s[t : t + 1, :])
        terms = jnp.concatenate([slope, w], 1).astype(bf16)
        pairs[c, t] = terms
        return jnp.dot(keys[block, :HD, :], terms[:, :BLK], preferred_element_type=f32)

    def patch(c):
        left = jnp.maximum(c - 1, 0)
        right = jnp.minimum(c + 1, COLS - 1)
        slots = []
        for i in range(2):
            slots.append((i, 2 * c + i, None))
            slots.append((i, 2 * c + 1 - i, None))
            slots.append((i, (ABOVE if i == 0 else BELOW) + c, (row > 0) if i == 0 else (row < ROWS - 1)))
            slots.append((i, 2 * left + i, c > 0))
            slots.append((i, 2 * right + i, c < COLS - 1))
            slots.append((i, GLOBAL, None))
        for q in range(COLS):
            slots.append((link_query[row, c, q], 2 * q + link_key[row, c, q], None))
        for i in range(2):
            pair = query[2 * c + i]
            zero = jnp.zeros_like(pair)
            both[2 * c + i] = jnp.concatenate([jnp.where(top_rows, pair, zero), jnp.where(top_rows, zero, pair)], 1)
        for t, (i, block, usable) in enumerate(slots):
            forward(2 * c + i, block, t, usable)
            if t >= WINDOW:
                i_s[t : t + 1, :] = jnp.full((1, BLK), i.astype(f32), f32)

        picks, deltas, parts = [], [], []
        for i in range(2):
            pick = i_s[...] == float(i)
            peak = jnp.where(pick, m_s[...], NEG)
            top = jnp.max(peak, axis=0, keepdims=True)
            part = jnp.where(pick, jnp.exp2((peak - top) * factor), 0.0)
            inverse = 1.0 / jnp.sum(l_s[...] * part, axis=0, keepdims=True)
            picks.append(pick)
            deltas.append(jnp.sum(a_s[...] * part, axis=0, keepdims=True) * inverse)
            parts.append(part * inverse)
        f_s[...] = parts[0] + parts[1]
        d_s[...] = jnp.where(picks[0], deltas[0], deltas[1])

        totals = [jnp.zeros((HD, BLK), f32), jnp.zeros((HD, BLK), f32)]
        for t, (i, block, _) in enumerate(slots):
            term = backward(c, block, t)
            if t < WINDOW:
                totals[i] = totals[i] + term
            else:
                totals[0] = totals[0] + jnp.where(i == 0, term, 0.0)
                totals[1] = totals[1] + jnp.where(i == 0, 0.0, term)
        send_dq[c] = (jnp.concatenate(totals, 0) * SCALE).astype(bf16)
        for way in range(2):
            term = turned_dot(both[2 * c + way], pairs[c, 6 * way + 2])
            halo_out[way, c] = (term * scale_rows).astype(bf16)
            halo_back(way, c).start()
        globe_acc[...] += turned_dot(both[2 * c], pairs[c, 5]) + turned_dot(both[2 * c + 1], pairs[c, 11])

    patch(col)
    own_dq = pltpu.make_async_copy(send_dq.at[col], got_dq.at[col], own_sem.at[3])
    own_dq.start()

    def patch_landed(step):
        scattered(1, send_qo, query, step).wait_recv()
        patch(shifted(row, col, step, -1))
        to_col(2, send_dq.at[shifted(row, col, step, -1)], got_dq.at[col], step, -1).start()

    loop(1, COLS, patch_landed)
    globe_acc[...] = globe_acc[...] * scale_rows

    @pl.when(row == 0)
    def _():
        loop(1, ROWS, lambda target: globe(target).wait_send())

    @pl.when(row != 0)
    def _():
        globe_back(row).start()

    @pl.when(row == 0)
    def _():
        loop(1, ROWS, lambda slot: globe_back(slot).wait_recv())
        total = globe_acc[...]
        for slot in range(1, ROWS):
            total = total + globe_in[slot]
        globe_acc[...] = total

    def terms_of(q):
        left = jnp.maximum(q - 1, 0)
        right = jnp.minimum(q + 1, COLS - 1)
        sides = []
        for j in range(2):
            before = pairs[left, 6 * j + 4]
            after = pairs[right, 6 * j + 3]
            none = jnp.zeros_like(before)
            near = (
                turned_dot(both[2 * q + j], pairs[q, 6 * j])
                + turned_dot(both[2 * q + 1 - j], pairs[q, 6 * (1 - j) + 1])
                + turned_dot(both[2 * left + j], jnp.where(q > 0, before, none))
                + turned_dot(both[2 * right + j], jnp.where(q < COLS - 1, after, none))
            )
            sides.append(near)
        total = jnp.concatenate(sides, 1)
        for c in range(COLS):
            term = pairs[c, WINDOW + q]
            none = jnp.zeros_like(term)
            first = link_key[row, c, q] == 0
            split = jnp.concatenate([jnp.where(first, term, none), jnp.where(first, none, term)], 0)
            total = total + turned_dot(both[2 * c + link_query[row, c, q]], split)
        for j in range(2):
            halo_back(1 - j, q).wait_recv()
            own = total[:, j * BLK : (j + 1) * BLK] * scale_rows + halo_in[j, q].astype(f32)
            if j == 0:
                own = own + jnp.where((q == 0) & (row == 0), globe_acc[...], 0.0)
            send_terms[q, j] = own.astype(bf16)

    def send_back(step):
        terms_of(shifted(row, col, step, 1))
        gather(3, send_terms, got_kv, step).start()

    loop(1, COLS, send_back)
    terms_of(col)
    own_back = pltpu.make_async_copy(send_terms.at[col], got_kv.at[col], own_sem.at[4])
    own_back.start()

    own_dq.wait()
    own_back.wait()

    def last(step):
        to_col(2, send_dq.at[col], got_dq.at[shifted(row, col, step, 1)], step, 1).wait_recv()
        gathered(3, send_terms, got_kv, step).wait_recv()
        scatter(0, send_kv, keys, step).wait_send()
        scatter(1, send_qo, query, step).wait_send()
        to_col(2, send_dq.at[shifted(row, col, step, -1)], got_dq.at[col], step, -1).wait_send()
        gather(3, send_terms, got_kv, step).wait_send()

    loop(1, COLS, last)

    def last_halo(c):
        for way in range(2):
            halo(way, c).wait_send()
            halo_back(way, c).wait_send()

    loop(0, COLS, last_halo)

    @pl.when(row != 0)
    def _():
        globe_back(row).wait_send()


def unpack(got_dq, got_kv, gq_out, gk_out, gv_out, wide):
    def turn(i, load, out):
        for h in range(HEADS):
            wide[h * HD : (h + 1) * HD, :] = load(h)
        for t in range(TILES):
            span = slice(t * BLK, (t + 1) * BLK)
            out[i, :, span] = wide[span, :].T.astype(bf16)

    for i in range(2):
        turn(i, lambda h: got_dq[h].astype(f32)[i * HD : (i + 1) * HD], gq_out)
        turn(i, lambda h: got_kv[h, i].astype(f32)[:HD], gk_out)
        turn(i, lambda h: got_kv[h, i].astype(f32)[HD:], gv_out)


VMEM = pl.BlockSpec(memory_space=pltpu.VMEM)
SMEM = pl.BlockSpec(memory_space=pltpu.SMEM)
DMA = pltpu.SemaphoreType.DMA
LIMIT = 61 * 1024 * 1024


def shape(dims, kind):
    return jax.ShapeDtypeStruct(dims, kind)


SCRATCH = [
    pltpu.VMEM((D, BLK), f32),
    pltpu.VMEM((D, BLK), f32),
    pltpu.VMEM((HEADS, 2, PAIR, BLK), bf16),
    pltpu.VMEM((HEADS, 2, PAIR, BLK), bf16),
    pltpu.VMEM((KEY_BLOCKS, PAIR, BLK), bf16),
    pltpu.VMEM((2 * COLS, PAIR, BLK), bf16),
    pltpu.VMEM((KEY_BLOCKS, BLK, PAIR), bf16),
    pltpu.VMEM((2 * COLS, PAIR, 2 * BLK), bf16),
    pltpu.VMEM((COLS, SLOTS, BLK, 2 * BLK), bf16),
    pltpu.VMEM((SLOTS, BLK, BLK), f32),
    pltpu.VMEM((SLOTS, BLK, BLK), f32),
    pltpu.VMEM((32, BLK), f32),
    pltpu.VMEM((32, BLK), f32),
    pltpu.VMEM((32, BLK), f32),
    pltpu.VMEM((32, BLK), f32),
    pltpu.VMEM((32, BLK), f32),
    pltpu.VMEM((32, BLK), f32),
    pltpu.VMEM((COLS, PAIR, BLK), bf16),
    pltpu.VMEM((COLS, 2, PAIR, BLK), bf16),
    pltpu.VMEM((2, COLS, PAIR, BLK), bf16),
    pltpu.VMEM((2, COLS, PAIR, BLK), bf16),
    pltpu.VMEM((PAIR, BLK), f32),
    pltpu.VMEM((ROWS, PAIR, BLK), f32),
    DMA((5,)),
    DMA((4, COLS)),
    DMA((4, COLS)),
    DMA((2, COLS)),
    DMA((2, COLS)),
    DMA((2, COLS)),
    DMA((2, COLS)),
    DMA((ROWS,)),
    DMA((ROWS,)),
]


def shards(queries, keys, values, dout, link_query, link_key):
    flat = [a.reshape(2, BLK, D) for a in (queries, keys, values, dout)]
    got_dq, got_kv = pl.pallas_call(
        attend,
        out_shape=(shape((HEADS, PAIR, BLK), bf16), shape((HEADS, 2, PAIR, BLK), bf16)),
        in_specs=[SMEM, SMEM] + [VMEM] * 4,
        out_specs=(VMEM, VMEM),
        scratch_shapes=SCRATCH,
        compiler_params=pltpu.CompilerParams(collective_id=0, has_side_effects=True, vmem_limit_bytes=LIMIT),
        name="attend",
    )(link_query, link_key, *flat)
    outs = pl.pallas_call(
        unpack,
        out_shape=(shape((2, BLK, D), bf16),) * 3,
        in_specs=[VMEM] * 2,
        out_specs=(VMEM,) * 3,
        scratch_shapes=[pltpu.VMEM((D, BLK), f32)],
        compiler_params=pltpu.CompilerParams(vmem_limit_bytes=LIMIT),
        name="unpack",
    )(got_dq, got_kv)
    return tuple(o.reshape(2, 1, BLK, D) for o in outs)


def solution(mesh):
    tiled = P("row", "col", None, None)
    return jax.shard_map(
        shards,
        mesh=mesh,
        in_specs=(tiled,) * 4 + (P(), P()),
        out_specs=(tiled,) * 3,
        check_vma=False,
    )
```

```python
import jax
import jax.numpy as jnp
from jax import lax
from jax.experimental import pallas as pl
from jax.experimental.pallas import tpu as pltpu
from jax.sharding import PartitionSpec as P

D = 1408
HEADS = 16
HD = D // HEADS
BLK = 128
ROWS = 8
COLS = 16
SIDE = 4
STRIDE = 5
PAIR = 2 * HD
TILES = D // BLK
ABOVE = 0
BELOW = COLS
GLOBAL = 2 * COLS
EDGES = GLOBAL + 1
AHEAD = 6
WINDOW = 12
SLOTS = WINDOW + COLS
SCALE = HD ** (-0.5)
LOG2E = 1.4426950408889634
NEG = -1e30
MESH = pl.DeviceIdType.MESH
f32 = jnp.float32
bf16 = jnp.bfloat16


def shifted(row, col, step, sign):
    core = lax.rem(row, 2)
    turn = lax.rem(step * STRIDE, COLS)
    first, second = turn // SIDE, lax.rem(turn, SIDE)
    dx = sign * (first * (1 - core) + (SIDE - second) * core)
    dz = sign * (second * (1 - core) + (SIDE - first) * core)
    x = lax.rem(col // SIDE + dx + SIDE, SIDE)
    z = lax.rem(lax.rem(col, SIDE) + dz + SIDE, SIDE)
    return x * SIDE + z


def loop(low, high, body):
    def step(i, carry):
        body(i)
        return carry

    lax.fori_loop(low, high, step, 0)


def turned_dot(a, b):
    return lax.dot_general(a, b, (((1,), (1,)), ((), ())), preferred_element_type=f32)


def attend(
    link_query, link_key, q_in, k_in, v_in, o_in, got_dq, got_kv,
    q_ref, k_ref, v_ref, o_ref, xt_a, xt_b, send_kv, send_qo, keys, edges, query, kvn, edges_n, both, pairs, p_s, u_s,
    m_s, l_s, a_s, f_s, d_s, i_s, send_dq, send_terms, halo_out, halo_in, globe_acc, globe_in,
    in_sem, own_sem, send_sem, recv_sem, halo_send, halo_recv, back_send, back_recv, globe_send, globe_recv,
):
    row = lax.axis_index("row")
    col = lax.axis_index("col")
    up = lax.rem(row + ROWS - 1, ROWS)
    down = lax.rem(row + 1, ROWS)
    factor = SCALE * LOG2E

    loads = [
        pltpu.make_async_copy(source, target, in_sem.at[n])
        for n, (source, target) in enumerate(((k_in, k_ref), (v_in, v_ref), (q_in, q_ref), (o_in, o_ref)))
    ]
    for load in loads:
        load.start()
    barrier = pltpu.get_barrier_semaphore()

    def greet(dest_row, dest_col):
        pl.semaphore_signal(barrier, inc=1, device_id=(dest_row, dest_col), device_id_type=MESH)

    loop(1, COLS, lambda step: greet(row, lax.rem(col + step, COLS)))
    loop(1, ROWS, lambda step: greet(lax.rem(row + step, ROWS), col))

    def to_col(kind, source_ref, target_ref, step, sign):
        return pltpu.make_async_remote_copy(
            src_ref=source_ref,
            dst_ref=target_ref,
            send_sem=send_sem.at[kind, step],
            recv_sem=recv_sem.at[kind, step],
            device_id=(row, shifted(row, col, step, sign)),
            device_id_type=MESH,
        )

    def scatter(kind, buffer, out, step):
        return to_col(kind, buffer.at[shifted(row, col, step, 1)], out.at[pl.ds(2 * col, 2)], step, 1)

    def scattered(kind, buffer, out, step):
        source = shifted(row, col, step, -1)
        return to_col(kind, buffer.at[source], out.at[pl.ds(2 * source, 2)], step, -1)

    def gather(kind, buffer, out, step):
        return to_col(kind, buffer.at[shifted(row, col, step, 1)], out.at[col], step, 1)

    def gathered(kind, buffer, out, step):
        source = shifted(row, col, step, -1)
        return to_col(kind, buffer.at[source], out.at[source], step, -1)

    def halo(way, source):
        return pltpu.make_async_remote_copy(
            src_ref=keys.at[2 * source + way],
            dst_ref=edges.at[(BELOW if way == 0 else ABOVE) + source],
            send_sem=halo_send.at[way, source],
            recv_sem=halo_recv.at[way, source],
            device_id=(up if way == 0 else down, col),
            device_id_type=MESH,
        )

    def halo_back(way, c):
        return pltpu.make_async_remote_copy(
            src_ref=halo_out.at[way, c],
            dst_ref=halo_in.at[1 - way, c],
            send_sem=back_send.at[way, c],
            recv_sem=back_recv.at[way, c],
            device_id=(up if way == 0 else down, col),
            device_id_type=MESH,
        )

    def globe(target):
        return pltpu.make_async_remote_copy(
            src_ref=keys.at[0],
            dst_ref=edges.at[GLOBAL],
            send_sem=globe_send.at[target],
            recv_sem=globe_recv.at[0],
            device_id=(target, col),
            device_id_type=MESH,
        )

    def globe_back(slot):
        return pltpu.make_async_remote_copy(
            src_ref=globe_acc,
            dst_ref=globe_in.at[slot],
            send_sem=globe_send.at[0],
            recv_sem=globe_recv.at[slot],
            device_id=(0, col),
            device_id_type=MESH,
        )

    def pack(first, second, buffer):
        def pack_block(i):
            for source, turned in ((first, xt_a), (second, xt_b)):
                for t in range(TILES):
                    span = slice(t * BLK, (t + 1) * BLK)
                    turned[span, :] = source[i, :, span].astype(f32).T
            for h in range(HEADS):
                span = slice(h * HD, (h + 1) * HD)
                buffer[h, i] = jnp.concatenate([xt_a[span, :], xt_b[span, :]], 0).astype(bf16)

        loop(0, 2, pack_block)

    def prepare(source, target, b):
        target[b] = source[b].astype(f32).T.astype(bf16)

    loads[0].wait()
    loads[1].wait()
    pack(k_ref, v_ref, send_kv)
    pl.semaphore_wait(barrier, COLS - 1 + ROWS - 1)
    loop(1, COLS, lambda step: scatter(0, send_kv, keys, step).start())
    own_kv = pltpu.make_async_copy(send_kv.at[col], keys.at[pl.ds(2 * col, 2)], own_sem.at[0])
    own_kv.start()
    loads[2].wait()
    loads[3].wait()
    pack(q_ref, o_ref, send_qo)
    own_qo = pltpu.make_async_copy(send_qo.at[col], query.at[pl.ds(2 * col, 2)], own_sem.at[1])
    own_qo.start()
    own_kv.wait()

    def pass_on(source):
        for way in range(2):
            halo(way, source).start()

        @pl.when((row == 0) & (source == 0))
        def _():
            loop(1, ROWS, lambda target: globe(target).start())

        for way in range(2):
            prepare(keys, kvn, 2 * source + way)

    def halo_landed(source):
        for way in range(2):
            halo(way, source).wait_recv()
        prepare(edges, edges_n, ABOVE + source)
        prepare(edges, edges_n, BELOW + source)

    pass_on(col)

    def landed(step):
        scattered(0, send_kv, keys, step).wait_recv()
        pass_on(shifted(row, col, step, -1))

    loop(1, COLS, landed)
    loop(1, 1 + AHEAD, lambda step: scatter(1, send_qo, query, step).start())

    @pl.when(row == 0)
    def _():
        own_globe = pltpu.make_async_copy(keys.at[0], edges.at[GLOBAL], own_sem.at[2])
        own_globe.start()
        own_globe.wait()

    @pl.when(row != 0)
    def _():
        globe(0).wait_recv()

    prepare(edges, edges_n, GLOBAL)
    own_qo.wait()

    top_rows = lax.broadcasted_iota(jnp.int32, (PAIR, BLK), 0) < HD
    scale_rows = jnp.where(top_rows, f32(SCALE), f32(1.0))
    globe_acc[...] = jnp.zeros(globe_acc.shape, f32)
    m_s[...] = jnp.full(m_s.shape, NEG, f32)
    l_s[...] = jnp.zeros(l_s.shape, f32)
    a_s[...] = jnp.zeros(a_s.shape, f32)
    i_s[...] = jnp.zeros(i_s.shape, f32)
    i_s[6:WINDOW, :] = jnp.ones((6, BLK), f32)
    i_s[SLOTS:, :] = jnp.full((32 - SLOTS, BLK), 2.0, f32)

    def forward(n, place, block, t, usable):
        su = jnp.dot(place[1][block], both[n], preferred_element_type=f32)
        s, u = su[:, :BLK], su[:, BLK:]
        m = jnp.max(s, axis=0, keepdims=True)
        p = jnp.exp2((s - m) * factor)
        p_s[t] = p
        u_s[t] = u
        m_s[t : t + 1, :] = m if usable is None else jnp.where(usable, m, NEG)
        l_s[t : t + 1, :] = jnp.sum(p, axis=0, keepdims=True)
        a_s[t : t + 1, :] = jnp.sum(p * u, axis=0, keepdims=True)

    def backward(c, place, block, t):
        w = p_s[t] * f_s[t : t + 1, :]
        slope = w * (u_s[t] - d_s[t : t + 1, :])
        terms = jnp.concatenate([slope, w], 1).astype(bf16)
        pairs[c, t] = terms
        return jnp.dot(place[0][block, :HD, :], terms[:, :BLK], preferred_element_type=f32)

    def patch(c):
        halo_landed(c)
        left = jnp.maximum(c - 1, 0)
        right = jnp.minimum(c + 1, COLS - 1)
        slots = []
        here, edge = (keys, kvn), (edges, edges_n)
        for i in range(2):
            outer = (row > 0) if i == 0 else (row < ROWS - 1)
            slots.append((i, here, 2 * c + i, None))
            slots.append((i, here, 2 * c + 1 - i, None))
            slots.append((i, edge, (ABOVE if i == 0 else BELOW) + c, outer))
            slots.append((i, here, 2 * left + i, c > 0))
            slots.append((i, here, 2 * right + i, c < COLS - 1))
            slots.append((i, edge, GLOBAL, None))
        for q in range(COLS):
            slots.append((link_query[row, c, q], here, 2 * q + link_key[row, c, q], None))
        for i in range(2):
            pair = query[2 * c + i]
            zero = jnp.zeros_like(pair)
            both[2 * c + i] = jnp.concatenate([jnp.where(top_rows, pair, zero), jnp.where(top_rows, zero, pair)], 1)
        for t, (i, place, block, usable) in enumerate(slots):
            forward(2 * c + i, place, block, t, usable)
            if t >= WINDOW:
                i_s[t : t + 1, :] = jnp.full((1, BLK), i.astype(f32), f32)

        picks, deltas, parts = [], [], []
        for i in range(2):
            pick = i_s[...] == float(i)
            peak = jnp.where(pick, m_s[...], NEG)
            top = jnp.max(peak, axis=0, keepdims=True)
            part = jnp.where(pick, jnp.exp2((peak - top) * factor), 0.0)
            inverse = 1.0 / jnp.sum(l_s[...] * part, axis=0, keepdims=True)
            picks.append(pick)
            deltas.append(jnp.sum(a_s[...] * part, axis=0, keepdims=True) * inverse)
            parts.append(part * inverse)
        f_s[...] = parts[0] + parts[1]
        d_s[...] = jnp.where(picks[0], deltas[0], deltas[1])

        totals = [jnp.zeros((HD, BLK), f32), jnp.zeros((HD, BLK), f32)]
        for t, (i, place, block, _) in enumerate(slots):
            term = backward(c, place, block, t)
            if t < WINDOW:
                totals[i] = totals[i] + term
            else:
                totals[0] = totals[0] + jnp.where(i == 0, term, 0.0)
                totals[1] = totals[1] + jnp.where(i == 0, 0.0, term)
        send_dq[c] = (jnp.concatenate(totals, 0) * SCALE).astype(bf16)
        for way in range(2):
            term = turned_dot(both[2 * c + way], pairs[c, 6 * way + 2])
            halo_out[way, c] = (term * scale_rows).astype(bf16)
            halo_back(way, c).start()
        globe_acc[...] += turned_dot(both[2 * c], pairs[c, 5]) + turned_dot(both[2 * c + 1], pairs[c, 11])

    patch(col)
    own_dq = pltpu.make_async_copy(send_dq.at[col], got_dq.at[col], own_sem.at[3])
    own_dq.start()

    def patch_landed(step):
        scattered(1, send_qo, query, step).wait_recv()
        patch(shifted(row, col, step, -1))
        to_col(2, send_dq.at[shifted(row, col, step, -1)], got_dq.at[col], step, -1).start()

    def patch_and_send(step):
        scatter(1, send_qo, query, step + AHEAD).start()
        patch_landed(step)

    loop(1, COLS - AHEAD, patch_and_send)
    loop(COLS - AHEAD, COLS, patch_landed)
    globe_acc[...] = globe_acc[...] * scale_rows

    @pl.when(row == 0)
    def _():
        loop(1, ROWS, lambda target: globe(target).wait_send())

    @pl.when(row != 0)
    def _():
        globe_back(row).start()

    def terms_of(q):
        left = jnp.maximum(q - 1, 0)
        right = jnp.minimum(q + 1, COLS - 1)
        sides = []
        for j in range(2):
            before = pairs[left, 6 * j + 4]
            after = pairs[right, 6 * j + 3]
            none = jnp.zeros_like(before)
            near = (
                turned_dot(both[2 * q + j], pairs[q, 6 * j])
                + turned_dot(both[2 * q + 1 - j], pairs[q, 6 * (1 - j) + 1])
                + turned_dot(both[2 * left + j], jnp.where(q > 0, before, none))
                + turned_dot(both[2 * right + j], jnp.where(q < COLS - 1, after, none))
            )
            sides.append(near)
        for c in range(COLS):
            term = pairs[c, WINDOW + q]
            term = turned_dot(both[2 * c + link_query[row, c, q]], term)
            first = link_key[row, c, q] == 0
            sides[0] = sides[0] + jnp.where(first, term, 0.0)
            sides[1] = sides[1] + jnp.where(first, 0.0, term)
        for j in range(2):
            halo_back(1 - j, q).wait_recv()
            own = sides[j] * scale_rows + halo_in[j, q].astype(f32)
            if j == 0:
                own = own + jnp.where((q == 0) & (row == 0), globe_acc[...], 0.0)
            send_terms[q, j] = own.astype(bf16)

    def send_back(step):
        q = shifted(row, col, step, 1)
        late = (row == 0) & (q == 0)
        terms_of(jnp.where(late, col, q))

        @pl.when(jnp.logical_not(late))
        def _():
            gather(3, send_terms, got_kv, step).start()

    loop(1, COLS, send_back)

    @pl.when(row == 0)
    def _():
        loop(1, ROWS, lambda slot: globe_back(slot).wait_recv())
        total = globe_acc[...]
        for slot in range(1, ROWS):
            total = total + globe_in[slot]
        globe_acc[...] = total

    terms_of(jnp.where(row == 0, 0, col))

    def send_late(step):
        @pl.when((row == 0) & (shifted(row, col, step, 1) == 0))
        def _():
            gather(3, send_terms, got_kv, step).start()

    loop(1, COLS, send_late)
    own_back = pltpu.make_async_copy(send_terms.at[col], got_kv.at[col], own_sem.at[4])
    own_back.start()

    own_dq.wait()
    own_back.wait()

    def last(step):
        to_col(2, send_dq.at[col], got_dq.at[shifted(row, col, step, 1)], step, 1).wait_recv()
        gathered(3, send_terms, got_kv, step).wait_recv()
        scatter(0, send_kv, keys, step).wait_send()
        scatter(1, send_qo, query, step).wait_send()
        to_col(2, send_dq.at[shifted(row, col, step, -1)], got_dq.at[col], step, -1).wait_send()
        gather(3, send_terms, got_kv, step).wait_send()

    loop(1, COLS, last)

    def last_halo(c):
        for way in range(2):
            halo(way, c).wait_send()
            halo_back(way, c).wait_send()

    loop(0, COLS, last_halo)

    @pl.when(row != 0)
    def _():
        globe_back(row).wait_send()


def unpack(got_dq, got_kv, gq_out, gk_out, gv_out, wide):
    def turn(i, load, out):
        for h in range(HEADS):
            wide[h * HD : (h + 1) * HD, :] = load(h)
        for t in range(TILES):
            span = slice(t * BLK, (t + 1) * BLK)
            out[i, :, span] = wide[span, :].T.astype(bf16)

    for i in range(2):
        turn(i, lambda h: got_dq[h].astype(f32)[i * HD : (i + 1) * HD], gq_out)
        turn(i, lambda h: got_kv[h, i].astype(f32)[:HD], gk_out)
        turn(i, lambda h: got_kv[h, i].astype(f32)[HD:], gv_out)


VMEM = pl.BlockSpec(memory_space=pltpu.VMEM)
ANY = pl.BlockSpec(memory_space=pl.ANY)
SMEM = pl.BlockSpec(memory_space=pltpu.SMEM)
DMA = pltpu.SemaphoreType.DMA
LIMIT = 61 * 1024 * 1024


def shape(dims, kind):
    return jax.ShapeDtypeStruct(dims, kind)


SCRATCH = [
    pltpu.VMEM((2, BLK, D), bf16),
    pltpu.VMEM((2, BLK, D), bf16),
    pltpu.VMEM((2, BLK, D), bf16),
    pltpu.VMEM((2, BLK, D), bf16),
    pltpu.VMEM((D, BLK), f32),
    pltpu.VMEM((D, BLK), f32),
    pltpu.VMEM((HEADS, 2, PAIR, BLK), bf16),
    pltpu.VMEM((HEADS, 2, PAIR, BLK), bf16),
    pltpu.VMEM((2 * COLS, PAIR, BLK), bf16),
    pltpu.VMEM((EDGES, PAIR, BLK), bf16),
    pltpu.VMEM((2 * COLS, PAIR, BLK), bf16),
    pltpu.VMEM((2 * COLS, BLK, PAIR), bf16),
    pltpu.VMEM((EDGES, BLK, PAIR), bf16),
    pltpu.VMEM((2 * COLS, PAIR, 2 * BLK), bf16),
    pltpu.VMEM((COLS, SLOTS, BLK, 2 * BLK), bf16),
    pltpu.VMEM((SLOTS, BLK, BLK), f32),
    pltpu.VMEM((SLOTS, BLK, BLK), f32),
    pltpu.VMEM((32, BLK), f32),
    pltpu.VMEM((32, BLK), f32),
    pltpu.VMEM((32, BLK), f32),
    pltpu.VMEM((32, BLK), f32),
    pltpu.VMEM((32, BLK), f32),
    pltpu.VMEM((32, BLK), f32),
    pltpu.VMEM((COLS, PAIR, BLK), bf16),
    pltpu.VMEM((COLS, 2, PAIR, BLK), bf16),
    pltpu.VMEM((2, COLS, PAIR, BLK), bf16),
    pltpu.VMEM((2, COLS, PAIR, BLK), bf16),
    pltpu.VMEM((PAIR, BLK), f32),
    pltpu.VMEM((ROWS, PAIR, BLK), f32),
    DMA((4,)),
    DMA((5,)),
    DMA((4, COLS)),
    DMA((4, COLS)),
    DMA((2, COLS)),
    DMA((2, COLS)),
    DMA((2, COLS)),
    DMA((2, COLS)),
    DMA((ROWS,)),
    DMA((ROWS,)),
]


def shards(queries, keys, values, dout, link_query, link_key):
    flat = [a.reshape(2, BLK, D) for a in (queries, keys, values, dout)]
    got_dq, got_kv = pl.pallas_call(
        attend,
        out_shape=(shape((HEADS, PAIR, BLK), bf16), shape((HEADS, 2, PAIR, BLK), bf16)),
        in_specs=[SMEM, SMEM] + [ANY] * 4,
        out_specs=(VMEM, VMEM),
        scratch_shapes=SCRATCH,
        compiler_params=pltpu.CompilerParams(collective_id=0, has_side_effects=True, vmem_limit_bytes=LIMIT),
        name="attend",
    )(link_query, link_key, *flat)
    outs = pl.pallas_call(
        unpack,
        out_shape=(shape((2, BLK, D), bf16),) * 3,
        in_specs=[VMEM] * 2,
        out_specs=(VMEM,) * 3,
        scratch_shapes=[pltpu.VMEM((D, BLK), f32)],
        compiler_params=pltpu.CompilerParams(vmem_limit_bytes=LIMIT),
        name="unpack",
    )(got_dq, got_kv)
    return tuple(o.reshape(2, 1, BLK, D) for o in outs)


def solution(mesh):
    tiled = P("row", "col", None, None)
    return jax.shard_map(
        shards,
        mesh=mesh,
        in_specs=(tiled,) * 4 + (P(), P()),
        out_specs=(tiled,) * 3,
        check_vma=False,
    )
```

```python
import jax
import jax.numpy as jnp
from jax import lax
from jax.experimental import pallas as pl
from jax.experimental.pallas import tpu as pltpu
from jax.sharding import PartitionSpec as P

D = 1408
HEADS = 16
HD = D // HEADS
BLK = 128
ROWS = 8
COLS = 16
SIDE = 4
STRIDE = 11
PAIR = 2 * HD
TILES = D // BLK
ABOVE = 0
BELOW = COLS
GLOBAL = 2 * COLS
EDGES = GLOBAL + 1
AHEAD = 6
WINDOW = 12
SLOTS = WINDOW + COLS
GROUPS = (BLK // 8, 8, BLK)
SCALE = HD ** (-0.5)
LOG2E = 1.4426950408889634
NEG = -1e30
MESH = pl.DeviceIdType.MESH
f32 = jnp.float32
bf16 = jnp.bfloat16


def shifted(col, step, sign):
    turn = lax.rem(step * STRIDE, COLS)
    dx = sign * (turn // SIDE)
    dz = sign * lax.rem(turn, SIDE)
    x = lax.rem(col // SIDE + dx + SIDE, SIDE)
    z = lax.rem(lax.rem(col, SIDE) + dz + SIDE, SIDE)
    return x * SIDE + z


def loop(low, high, body):
    def step(i, carry):
        body(i)
        return carry

    lax.fori_loop(low, high, step, 0)


def turned_dot(a, b):
    return lax.dot_general(a, b, (((1,), (1,)), ((), ())), preferred_element_type=f32)


def attend(
    link_query, link_key, q_in, k_in, v_in, o_in, got_dq, got_kv,
    first_ref, second_ref, xt_a, xt_b, send_kv, send_qo, keys, edges, query, kvn, edges_n, both, pairs, p_s, u_s,
    m_s, l_s, a_s, f_s, d_s, send_dq, send_terms, halo_out, halo_in, globe_acc, globe_in,
    in_sem, own_sem, send_sem, recv_sem, halo_send, halo_recv, back_send, back_recv, globe_send, globe_recv,
):
    row = lax.axis_index("row")
    col = lax.axis_index("col")
    up = lax.rem(row + ROWS - 1, ROWS)
    down = lax.rem(row + 1, ROWS)
    factor = SCALE * LOG2E

    loads = [
        pltpu.make_async_copy(source, target, in_sem.at[n])
        for n, (source, target) in enumerate(((k_in, first_ref), (v_in, second_ref), (q_in, first_ref), (o_in, second_ref)))
    ]
    for load in loads[:2]:
        load.start()
    barrier = pltpu.get_barrier_semaphore()

    def greet(dest_row, dest_col):
        pl.semaphore_signal(barrier, inc=1, device_id=(dest_row, dest_col), device_id_type=MESH)

    loop(1, COLS, lambda step: greet(row, lax.rem(col + step, COLS)))
    loop(1, ROWS, lambda step: greet(lax.rem(row + step, ROWS), col))

    def to_col(kind, source_ref, target_ref, step, sign):
        return pltpu.make_async_remote_copy(
            src_ref=source_ref,
            dst_ref=target_ref,
            send_sem=send_sem.at[kind, step],
            recv_sem=recv_sem.at[kind, step],
            device_id=(row, shifted(col, step, sign)),
            device_id_type=MESH,
        )

    def scatter(kind, buffer, out, step):
        return to_col(kind, buffer.at[shifted(col, step, 1)], out.at[pl.ds(2 * col, 2)], step, 1)

    def scattered(kind, buffer, out, step):
        source = shifted(col, step, -1)
        return to_col(kind, buffer.at[source], out.at[pl.ds(2 * source, 2)], step, -1)

    def gather(kind, buffer, out, step):
        return to_col(kind, buffer.at[shifted(col, step, 1)], out.at[col], step, 1)

    def gathered(kind, buffer, out, step):
        source = shifted(col, step, -1)
        return to_col(kind, buffer.at[source], out.at[source], step, -1)

    def halo(way, source):
        return pltpu.make_async_remote_copy(
            src_ref=keys.at[2 * source + way],
            dst_ref=edges.at[(BELOW if way == 0 else ABOVE) + source],
            send_sem=halo_send.at[way, source],
            recv_sem=halo_recv.at[way, source],
            device_id=(up if way == 0 else down, col),
            device_id_type=MESH,
        )

    def halo_back(way, c):
        return pltpu.make_async_remote_copy(
            src_ref=halo_out.at[way, c],
            dst_ref=halo_in.at[1 - way, c],
            send_sem=back_send.at[way, c],
            recv_sem=back_recv.at[way, c],
            device_id=(up if way == 0 else down, col),
            device_id_type=MESH,
        )

    def globe(target):
        return pltpu.make_async_remote_copy(
            src_ref=keys.at[0],
            dst_ref=edges.at[GLOBAL],
            send_sem=globe_send.at[target],
            recv_sem=globe_recv.at[0],
            device_id=(target, col),
            device_id_type=MESH,
        )

    def globe_back(slot):
        return pltpu.make_async_remote_copy(
            src_ref=globe_acc,
            dst_ref=globe_in.at[slot],
            send_sem=globe_send.at[0],
            recv_sem=globe_recv.at[slot],
            device_id=(0, col),
            device_id_type=MESH,
        )

    def pack(first, second, buffer):
        def pack_block(i):
            for source, turned in ((first, xt_a), (second, xt_b)):
                for t in range(TILES):
                    span = slice(t * BLK, (t + 1) * BLK)
                    turned[span, :] = source[i, :, span].astype(f32).T
            for h in range(HEADS):
                span = slice(h * HD, (h + 1) * HD)
                buffer[h, i] = jnp.concatenate([xt_a[span, :], xt_b[span, :]], 0).astype(bf16)

        loop(0, 2, pack_block)

    def prepare(source, target, b):
        target[b] = source[b].astype(f32).T.astype(bf16)

    loads[0].wait()
    loads[1].wait()
    pack(first_ref, second_ref, send_kv)
    loads[2].start()
    loads[3].start()
    pl.semaphore_wait(barrier, COLS - 1 + ROWS - 1)
    loop(1, COLS, lambda step: scatter(0, send_kv, keys, step).start())
    own_kv = pltpu.make_async_copy(send_kv.at[col], keys.at[pl.ds(2 * col, 2)], own_sem.at[0])
    own_kv.start()
    loads[2].wait()
    loads[3].wait()
    pack(first_ref, second_ref, send_qo)
    own_qo = pltpu.make_async_copy(send_qo.at[col], query.at[pl.ds(2 * col, 2)], own_sem.at[1])
    own_qo.start()
    own_kv.wait()

    def pass_on(source):
        for way in range(2):
            halo(way, source).start()

        @pl.when((row == 0) & (source == 0))
        def _():
            loop(1, ROWS, lambda target: globe(target).start())

        for way in range(2):
            prepare(keys, kvn, 2 * source + way)

    def halo_landed(source):
        for way in range(2):
            halo(way, source).wait_recv()
        prepare(edges, edges_n, ABOVE + source)
        prepare(edges, edges_n, BELOW + source)

    pass_on(col)

    def landed(step):
        scattered(0, send_kv, keys, step).wait_recv()
        pass_on(shifted(col, step, -1))

    loop(1, COLS, landed)
    loop(1, 1 + AHEAD, lambda step: scatter(1, send_qo, query, step).start())

    @pl.when(row == 0)
    def _():
        own_globe = pltpu.make_async_copy(keys.at[0], edges.at[GLOBAL], own_sem.at[2])
        own_globe.start()
        own_globe.wait()

    @pl.when(row != 0)
    def _():
        globe(0).wait_recv()

    prepare(edges, edges_n, GLOBAL)
    own_qo.wait()

    top_rows = lax.broadcasted_iota(jnp.int32, (PAIR, BLK), 0) < HD
    scale_rows = jnp.where(top_rows, f32(SCALE), f32(1.0))
    globe_acc[...] = jnp.zeros(globe_acc.shape, f32)
    def forward(n, place, block, t, usable):
        su = jnp.dot(place[1][block], both[n], preferred_element_type=f32)
        s, u = su[:, :BLK], su[:, BLK:]
        s, u = s.reshape(GROUPS), u.reshape(GROUPS)
        m = jnp.max(s, axis=0)
        p = jnp.exp2((s - m) * factor)
        p_s[t] = p
        u_s[t] = u
        m_s[t] = m if usable is None else jnp.where(usable, m, NEG)
        l_s[t] = jnp.sum(p, axis=0)
        a_s[t] = jnp.sum(p * u, axis=0)

    def backward(c, place, block, t, half):
        v = t + SLOTS * half
        w = p_s[v] * f_s[v]
        slope = w * (u_s[v] - d_s[v])
        terms = jnp.concatenate([slope.reshape(BLK, BLK), w.reshape(BLK, BLK)], 1).astype(bf16)
        pairs[c, t] = terms
        return jnp.dot(place[0][block, :HD, :], terms[:, :BLK], preferred_element_type=f32)

    def patch(c, half=0):
        left = jnp.maximum(c - 1, 0)
        right = jnp.minimum(c + 1, COLS - 1)
        slots = []
        here, edge = (keys, kvn), (edges, edges_n)
        for i in range(2):
            outer = (row > 0) if i == 0 else (row < ROWS - 1)
            slots.append((i, here, 2 * c + i, None))
            slots.append((i, here, 2 * c + 1 - i, None))
            slots.append((i, edge, (ABOVE if i == 0 else BELOW) + c, outer))
            slots.append((i, here, 2 * left + i, c > 0))
            slots.append((i, here, 2 * right + i, c < COLS - 1))
            slots.append((i, edge, GLOBAL, None))
        for q in range(COLS):
            slots.append((link_query[row, c, q], here, 2 * q + link_key[row, c, q], None))
        for i in range(2):
            pair = query[2 * c + i]
            zero = jnp.zeros_like(pair)
            both[2 * c + i] = jnp.concatenate([jnp.where(top_rows, pair, zero), jnp.where(top_rows, zero, pair)], 1)
        for t, (i, place, block, usable) in enumerate(slots):
            forward(2 * c + i, place, block, t + SLOTS * half, usable)

        def of(i, here, other):
            if isinstance(i, int):
                return here if i == 0 else other
            return jnp.where(i == 0, here, other)

        tops = [jnp.full((8, BLK), NEG, f32)] * 2
        for t, (i, _, _, _) in enumerate(slots):
            m = m_s[t + SLOTS * half]
            tops = [jnp.maximum(tops[0], of(i, m, NEG)), jnp.maximum(tops[1], of(i, NEG, m))]
        tops = [jnp.broadcast_to(jnp.max(top, axis=0, keepdims=True), (8, BLK)) for top in tops]
        sums, deltas = [jnp.zeros((8, BLK), f32)] * 2, [jnp.zeros((8, BLK), f32)] * 2
        for t, (i, _, _, _) in enumerate(slots):
            part = jnp.exp2((m_s[t + SLOTS * half] - of(i, tops[0], tops[1])) * factor)
            f_s[t + SLOTS * half] = part
            mass, pull = l_s[t + SLOTS * half] * part, a_s[t + SLOTS * half] * part
            sums = [sums[0] + of(i, mass, 0.0), sums[1] + of(i, 0.0, mass)]
            deltas = [deltas[0] + of(i, pull, 0.0), deltas[1] + of(i, 0.0, pull)]
        inverses = [1.0 / jnp.sum(total, axis=0, keepdims=True) for total in sums]
        deltas = [
            jnp.broadcast_to(jnp.sum(pull, axis=0, keepdims=True) * inverse, (8, BLK))
            for pull, inverse in zip(deltas, inverses)
        ]
        inverses = [jnp.broadcast_to(inverse, (8, BLK)) for inverse in inverses]
        for t, (i, _, _, _) in enumerate(slots):
            f_s[t + SLOTS * half] = f_s[t + SLOTS * half] * of(i, inverses[0], inverses[1])
            d_s[t + SLOTS * half] = of(i, deltas[0], deltas[1])

        totals = [jnp.zeros((HD, BLK), f32), jnp.zeros((HD, BLK), f32)]
        for t, (i, place, block, _) in enumerate(slots):
            term = backward(c, place, block, t, half)
            if t < WINDOW:
                totals[i] = totals[i] + term
            else:
                totals[0] = totals[0] + jnp.where(i == 0, term, 0.0)
                totals[1] = totals[1] + jnp.where(i == 0, 0.0, term)
        send_dq[c] = (jnp.concatenate(totals, 0) * SCALE).astype(bf16)
        for way in range(2):
            term = turned_dot(both[2 * c + way], pairs[c, 6 * way + 2])
            halo_out[way, c] = (term * scale_rows).astype(bf16)
        globe_acc[...] += turned_dot(both[2 * c], pairs[c, 5]) + turned_dot(both[2 * c + 1], pairs[c, 11])

    def patch_here(step):
        scattered(1, send_qo, query, step).wait_recv()
        halo_landed(shifted(col, step, -1))

        @pl.when(step + AHEAD < COLS)
        def _():
            scatter(1, send_qo, query, step + AHEAD).start()

    def patch_away(step):
        source = shifted(col, step, -1)
        to_col(2, send_dq.at[source], got_dq.at[col], step, -1).start()
        for way in range(2):
            halo_back(way, source).start()

    halo_landed(col)
    patch(col)
    own_dq = pltpu.make_async_copy(send_dq.at[col], got_dq.at[col], own_sem.at[3])
    own_dq.start()
    for way in range(2):
        halo_back(way, col).start()

    def two_patches(k):
        patch_here(2 * k + 1)
        patch_here(2 * k + 2)
        patch(shifted(col, 2 * k + 1, -1), 0)
        patch(shifted(col, 2 * k + 2, -1), 1)
        patch_away(2 * k + 1)
        patch_away(2 * k + 2)

    loop(0, COLS // 2 - 1, two_patches)
    patch_here(COLS - 1)
    patch(shifted(col, COLS - 1, -1))
    patch_away(COLS - 1)
    globe_acc[...] = globe_acc[...] * scale_rows

    @pl.when(row == 0)
    def _():
        loop(1, ROWS, lambda target: globe(target).wait_send())

    @pl.when(row != 0)
    def _():
        globe_back(row).start()

    def terms_of(q):
        left = jnp.maximum(q - 1, 0)
        right = jnp.minimum(q + 1, COLS - 1)
        sides = []
        for j in range(2):
            before = pairs[left, 6 * j + 4]
            after = pairs[right, 6 * j + 3]
            none = jnp.zeros_like(before)
            near = (
                turned_dot(both[2 * q + j], pairs[q, 6 * j])
                + turned_dot(both[2 * q + 1 - j], pairs[q, 6 * (1 - j) + 1])
                + turned_dot(both[2 * left + j], jnp.where(q > 0, before, none))
                + turned_dot(both[2 * right + j], jnp.where(q < COLS - 1, after, none))
            )
            sides.append(near)
        for c in range(COLS):
            term = pairs[c, WINDOW + q]
            term = turned_dot(both[2 * c + link_query[row, c, q]], term)
            first = link_key[row, c, q] == 0
            sides[0] = sides[0] + jnp.where(first, term, 0.0)
            sides[1] = sides[1] + jnp.where(first, 0.0, term)
        for j in range(2):
            halo_back(1 - j, q).wait_recv()
            own = sides[j] * scale_rows + halo_in[j, q].astype(f32)
            if j == 0:
                own = own + jnp.where((q == 0) & (row == 0), globe_acc[...], 0.0)
            send_terms[q, j] = own.astype(bf16)

    def send_back(step):
        q = shifted(col, step, 1)
        late = (row == 0) & (q == 0)
        terms_of(jnp.where(late, col, q))

        @pl.when(jnp.logical_not(late))
        def _():
            gather(3, send_terms, got_kv, step).start()

    loop(1, COLS, send_back)

    @pl.when(row == 0)
    def _():
        loop(1, ROWS, lambda slot: globe_back(slot).wait_recv())
        total = globe_acc[...]
        for slot in range(1, ROWS):
            total = total + globe_in[slot]
        globe_acc[...] = total

    terms_of(jnp.where(row == 0, 0, col))

    def send_late(step):
        @pl.when((row == 0) & (shifted(col, step, 1) == 0))
        def _():
            gather(3, send_terms, got_kv, step).start()

    loop(1, COLS, send_late)
    own_back = pltpu.make_async_copy(send_terms.at[col], got_kv.at[col], own_sem.at[4])
    own_back.start()

    own_dq.wait()
    own_back.wait()

    def last(step):
        to_col(2, send_dq.at[col], got_dq.at[shifted(col, step, 1)], step, 1).wait_recv()
        gathered(3, send_terms, got_kv, step).wait_recv()
        scatter(0, send_kv, keys, step).wait_send()
        scatter(1, send_qo, query, step).wait_send()
        to_col(2, send_dq.at[shifted(col, step, -1)], got_dq.at[col], step, -1).wait_send()
        gather(3, send_terms, got_kv, step).wait_send()

    loop(1, COLS, last)

    def last_halo(c):
        for way in range(2):
            halo(way, c).wait_send()
            halo_back(way, c).wait_send()

    loop(0, COLS, last_halo)

    @pl.when(row != 0)
    def _():
        globe_back(row).wait_send()


def unpack(got_dq, got_kv, gq_out, gk_out, gv_out, dq, kv, wide, turned, in_sem, out_sem):
    loads = [pltpu.make_async_copy(got_dq, dq, in_sem.at[0])]
    loads += [pltpu.make_async_copy(got_kv.at[:, i], kv.at[i], in_sem.at[1 + i]) for i in range(2)]
    for load in loads:
        load.start()
    stores = []

    def turn(n, i, load, out):
        for h in range(HEADS):
            wide[n, h * HD : (h + 1) * HD, :] = load(h)
        for t in range(TILES):
            span = slice(t * BLK, (t + 1) * BLK)
            turned[n, :, span] = wide[n, span, :].T.astype(bf16)
        stores.append(pltpu.make_async_copy(turned.at[n], out.at[i], out_sem.at[n]))
        stores[-1].start()

    loads[0].wait()
    for i in range(2):
        turn(i, i, lambda h: dq[h].astype(f32)[i * HD : (i + 1) * HD], gq_out)
    for i in range(2):
        loads[1 + i].wait()
        turn(2 + 2 * i, i, lambda h: kv[i, h].astype(f32)[:HD], gk_out)
        turn(3 + 2 * i, i, lambda h: kv[i, h].astype(f32)[HD:], gv_out)
    for store in stores:
        store.wait()


VMEM = pl.BlockSpec(memory_space=pltpu.VMEM)
ANY = pl.BlockSpec(memory_space=pl.ANY)
SMEM = pl.BlockSpec(memory_space=pltpu.SMEM)
DMA = pltpu.SemaphoreType.DMA
LIMIT = 61 * 1024 * 1024


def shape(dims, kind):
    return jax.ShapeDtypeStruct(dims, kind)


SCRATCH = [
    pltpu.VMEM((2, BLK, D), bf16),
    pltpu.VMEM((2, BLK, D), bf16),
    pltpu.VMEM((D, BLK), f32),
    pltpu.VMEM((D, BLK), f32),
    pltpu.VMEM((HEADS, 2, PAIR, BLK), bf16),
    pltpu.VMEM((HEADS, 2, PAIR, BLK), bf16),
    pltpu.VMEM((2 * COLS, PAIR, BLK), bf16),
    pltpu.VMEM((EDGES, PAIR, BLK), bf16),
    pltpu.VMEM((2 * COLS, PAIR, BLK), bf16),
    pltpu.VMEM((2 * COLS, BLK, PAIR), bf16),
    pltpu.VMEM((EDGES, BLK, PAIR), bf16),
    pltpu.VMEM((2 * COLS, PAIR, 2 * BLK), bf16),
    pltpu.VMEM((COLS, SLOTS, BLK, 2 * BLK), bf16),
    pltpu.VMEM((2 * SLOTS,) + GROUPS, f32),
    pltpu.VMEM((2 * SLOTS,) + GROUPS, f32),
    pltpu.VMEM((2 * SLOTS, 8, BLK), f32),
    pltpu.VMEM((2 * SLOTS, 8, BLK), f32),
    pltpu.VMEM((2 * SLOTS, 8, BLK), f32),
    pltpu.VMEM((2 * SLOTS, 8, BLK), f32),
    pltpu.VMEM((2 * SLOTS, 8, BLK), f32),
    pltpu.VMEM((COLS, PAIR, BLK), bf16),
    pltpu.VMEM((COLS, 2, PAIR, BLK), bf16),
    pltpu.VMEM((2, COLS, PAIR, BLK), bf16),
    pltpu.VMEM((2, COLS, PAIR, BLK), bf16),
    pltpu.VMEM((PAIR, BLK), f32),
    pltpu.VMEM((ROWS, PAIR, BLK), f32),
    DMA((4,)),
    DMA((5,)),
    DMA((4, COLS)),
    DMA((4, COLS)),
    DMA((2, COLS)),
    DMA((2, COLS)),
    DMA((2, COLS)),
    DMA((2, COLS)),
    DMA((ROWS,)),
    DMA((ROWS,)),
]


def shards(queries, keys, values, dout, link_query, link_key):
    flat = [a.reshape(2, BLK, D) for a in (queries, keys, values, dout)]
    got_dq, got_kv = pl.pallas_call(
        attend,
        out_shape=(shape((HEADS, PAIR, BLK), bf16), shape((HEADS, 2, PAIR, BLK), bf16)),
        in_specs=[SMEM, SMEM] + [ANY] * 4,
        out_specs=(ANY, ANY),
        scratch_shapes=SCRATCH,
        compiler_params=pltpu.CompilerParams(collective_id=0, has_side_effects=True, vmem_limit_bytes=LIMIT),
        name="attend",
    )(link_query, link_key, *flat)
    outs = pl.pallas_call(
        unpack,
        out_shape=(shape((2, BLK, D), bf16),) * 3,
        in_specs=[ANY] * 2,
        out_specs=(ANY,) * 3,
        scratch_shapes=[
            pltpu.VMEM((HEADS, PAIR, BLK), bf16),
            pltpu.VMEM((2, HEADS, PAIR, BLK), bf16),
            pltpu.VMEM((6, D, BLK), f32),
            pltpu.VMEM((6, BLK, D), bf16),
            DMA((3,)),
            DMA((6,)),
        ],
        compiler_params=pltpu.CompilerParams(vmem_limit_bytes=LIMIT),
        name="unpack",
    )(got_dq, got_kv)
    return tuple(o.reshape(2, 1, BLK, D) for o in outs)


def solution(mesh):
    tiled = P("row", "col", None, None)
    return jax.shard_map(
        shards,
        mesh=mesh,
        in_specs=(tiled,) * 4 + (P(), P()),
        out_specs=(tiled,) * 3,
        check_vma=False,
    )
```

```python
import jax
import jax.numpy as jnp
from jax import lax
from jax.experimental import pallas as pl
from jax.experimental.pallas import tpu as pltpu
from jax.sharding import PartitionSpec as P

D = 1408
HEADS = 16
HD = D // HEADS
BLK = 128
ROWS = 8
COLS = 16
SIDE = 4
STRIDE = 11
PAIR = 2 * HD
TILES = D // BLK
ABOVE = 0
BELOW = COLS
GLOBAL = 2 * COLS
EDGES = GLOBAL + 1
AHEAD = 6
WINDOW = 12
SLOTS = WINDOW + COLS
GROUPS = (BLK // 8, 8, BLK)
SCALE = HD ** (-0.5)
LOG2E = 1.4426950408889634
NEG = -1e30
MESH = pl.DeviceIdType.MESH
f32 = jnp.float32
bf16 = jnp.bfloat16


def shifted(col, step, sign):
    turn = lax.rem(step * STRIDE, COLS)
    dx = sign * (turn // SIDE)
    dz = sign * lax.rem(turn, SIDE)
    x = lax.rem(col // SIDE + dx + SIDE, SIDE)
    z = lax.rem(lax.rem(col, SIDE) + dz + SIDE, SIDE)
    return x * SIDE + z


def loop(low, high, body):
    def step(i, carry):
        body(i)
        return carry

    lax.fori_loop(low, high, step, 0)


def turned_dot(a, b):
    return lax.dot_general(a, b, (((1,), (1,)), ((), ())), preferred_element_type=f32)


def attend(
    link_query, link_key, q_in, k_in, v_in, o_in, got_dq, got_kv,
    first_ref, second_ref, xt_a, xt_b, send_kv, send_qo, keys, edges, query, kvn, edges_n, both, pairs, p_s, u_s,
    m_s, l_s, a_s, f_s, d_s, send_dq, send_terms, halo_out, halo_in, globe_acc, globe_in,
    in_sem, own_sem, send_sem, recv_sem, halo_send, halo_recv, back_send, back_recv, globe_send, globe_recv,
):
    row = lax.axis_index("row")
    col = lax.axis_index("col")
    up = lax.rem(row + ROWS - 1, ROWS)
    down = lax.rem(row + 1, ROWS)
    factor = SCALE * LOG2E

    loads = [
        pltpu.make_async_copy(source, target, in_sem.at[n])
        for n, (source, target) in enumerate(((k_in, first_ref), (v_in, second_ref), (q_in, first_ref), (o_in, second_ref)))
    ]
    for load in loads[:2]:
        load.start()
    barrier = pltpu.get_barrier_semaphore()

    def greet(dest_row, dest_col):
        pl.semaphore_signal(barrier, inc=1, device_id=(dest_row, dest_col), device_id_type=MESH)

    loop(1, COLS, lambda step: greet(row, lax.rem(col + step, COLS)))
    loop(1, ROWS, lambda step: greet(lax.rem(row + step, ROWS), col))

    def to_col(kind, source_ref, target_ref, step, sign):
        return pltpu.make_async_remote_copy(
            src_ref=source_ref,
            dst_ref=target_ref,
            send_sem=send_sem.at[kind, step],
            recv_sem=recv_sem.at[kind, step],
            device_id=(row, shifted(col, step, sign)),
            device_id_type=MESH,
        )

    def scatter_key(way, step):
        return to_col(4 * way, send_kv.at[shifted(col, step, 1), way], keys.at[2 * col + way], step, 1)

    def scattered_key(way, step):
        source = shifted(col, step, -1)
        return to_col(4 * way, send_kv.at[source, way], keys.at[2 * source + way], step, -1)

    def scatter(kind, buffer, out, step):
        return to_col(kind, buffer.at[shifted(col, step, 1)], out.at[pl.ds(2 * col, 2)], step, 1)

    def scattered(kind, buffer, out, step):
        source = shifted(col, step, -1)
        return to_col(kind, buffer.at[source], out.at[pl.ds(2 * source, 2)], step, -1)

    def gather(kind, buffer, out, step):
        return to_col(kind, buffer.at[shifted(col, step, 1)], out.at[col], step, 1)

    def gathered(kind, buffer, out, step):
        source = shifted(col, step, -1)
        return to_col(kind, buffer.at[source], out.at[source], step, -1)

    def halo(way, source):
        return pltpu.make_async_remote_copy(
            src_ref=keys.at[2 * source + way],
            dst_ref=edges.at[(BELOW if way == 0 else ABOVE) + source],
            send_sem=halo_send.at[way, source],
            recv_sem=halo_recv.at[way, source],
            device_id=(up if way == 0 else down, col),
            device_id_type=MESH,
        )

    def halo_back(way, c):
        return pltpu.make_async_remote_copy(
            src_ref=halo_out.at[way, c],
            dst_ref=halo_in.at[1 - way, c],
            send_sem=back_send.at[way, c],
            recv_sem=back_recv.at[way, c],
            device_id=(up if way == 0 else down, col),
            device_id_type=MESH,
        )

    def globe(target):
        return pltpu.make_async_remote_copy(
            src_ref=keys.at[0],
            dst_ref=edges.at[GLOBAL],
            send_sem=globe_send.at[target],
            recv_sem=globe_recv.at[0],
            device_id=(target, col),
            device_id_type=MESH,
        )

    def globe_back(slot):
        return pltpu.make_async_remote_copy(
            src_ref=globe_acc,
            dst_ref=globe_in.at[slot],
            send_sem=globe_send.at[0],
            recv_sem=globe_recv.at[slot],
            device_id=(0, col),
            device_id_type=MESH,
        )

    def pack(first, second, buffer):
        def pack_block(i):
            for source, turned in ((first, xt_a), (second, xt_b)):
                for t in range(TILES):
                    span = slice(t * BLK, (t + 1) * BLK)
                    turned[span, :] = source[i, :, span].astype(f32).T
            for h in range(HEADS):
                span = slice(h * HD, (h + 1) * HD)
                buffer[h, i] = jnp.concatenate([xt_a[span, :], xt_b[span, :]], 0).astype(bf16)

        loop(0, 2, pack_block)

    def prepare(source, target, b):
        target[b] = source[b].astype(f32).T.astype(bf16)

    loads[0].wait()
    loads[1].wait()
    pack(first_ref, second_ref, send_kv)
    loads[2].start()
    loads[3].start()
    pl.semaphore_wait(barrier, COLS - 1 + ROWS - 1)
    for way in range(2):
        loop(1, COLS, lambda step: scatter_key(way, step).start())
    own_kv = pltpu.make_async_copy(send_kv.at[col], keys.at[pl.ds(2 * col, 2)], own_sem.at[0])
    own_kv.start()
    loads[2].wait()
    loads[3].wait()
    pack(first_ref, second_ref, send_qo)
    own_qo = pltpu.make_async_copy(send_qo.at[col], query.at[pl.ds(2 * col, 2)], own_sem.at[1])
    own_qo.start()
    own_kv.wait()

    def pass_on(way, source):
        halo(way, source).start()
        if way == 0:

            @pl.when((row == 0) & (source == 0))
            def _():
                loop(1, ROWS, lambda target: globe(target).start())

        prepare(keys, kvn, 2 * source + way)

    def halo_landed(source):
        for way in range(2):
            halo(way, source).wait_recv()
        prepare(edges, edges_n, ABOVE + source)
        prepare(edges, edges_n, BELOW + source)

    for way in range(2):
        pass_on(way, col)

        def landed(step):
            scattered_key(way, step).wait_recv()
            pass_on(way, shifted(col, step, -1))

        loop(1, COLS, landed)

    loop(1, 1 + AHEAD, lambda step: scatter(1, send_qo, query, step).start())

    @pl.when(row == 0)
    def _():
        own_globe = pltpu.make_async_copy(keys.at[0], edges.at[GLOBAL], own_sem.at[2])
        own_globe.start()
        own_globe.wait()

    @pl.when(row != 0)
    def _():
        globe(0).wait_recv()

    prepare(edges, edges_n, GLOBAL)
    own_qo.wait()

    top_rows = lax.broadcasted_iota(jnp.int32, (PAIR, BLK), 0) < HD
    scale_rows = jnp.where(top_rows, f32(SCALE), f32(1.0))
    globe_acc[...] = jnp.zeros(globe_acc.shape, f32)
    def forward(n, place, block, t, usable):
        su = jnp.dot(place[1][block], both[n], preferred_element_type=f32)
        s, u = su[:, :BLK], su[:, BLK:]
        s, u = s.reshape(GROUPS), u.reshape(GROUPS)
        m = jnp.max(s, axis=0)
        p = jnp.exp2((s - m) * factor)
        p_s[t] = p
        u_s[t] = u
        m_s[t] = m if usable is None else jnp.where(usable, m, NEG)
        l_s[t] = jnp.sum(p, axis=0)
        a_s[t] = jnp.sum(p * u, axis=0)

    def backward(c, place, block, t, half):
        v = t + SLOTS * half
        w = p_s[v] * f_s[v]
        slope = w * (u_s[v] - d_s[v])
        terms = jnp.concatenate([slope.reshape(BLK, BLK), w.reshape(BLK, BLK)], 1).astype(bf16)
        pairs[c, t] = terms
        return jnp.dot(place[0][block, :HD, :], terms[:, :BLK], preferred_element_type=f32)

    def patch(c, half=0):
        left = jnp.maximum(c - 1, 0)
        right = jnp.minimum(c + 1, COLS - 1)
        slots = []
        here, edge = (keys, kvn), (edges, edges_n)
        for i in range(2):
            outer = (row > 0) if i == 0 else (row < ROWS - 1)
            slots.append((i, here, 2 * c + i, None))
            slots.append((i, here, 2 * c + 1 - i, None))
            slots.append((i, edge, (ABOVE if i == 0 else BELOW) + c, outer))
            slots.append((i, here, 2 * left + i, c > 0))
            slots.append((i, here, 2 * right + i, c < COLS - 1))
            slots.append((i, edge, GLOBAL, None))
        for q in range(COLS):
            slots.append((link_query[row, c, q], here, 2 * q + link_key[row, c, q], None))
        for i in range(2):
            pair = query[2 * c + i]
            zero = jnp.zeros_like(pair)
            both[2 * c + i] = jnp.concatenate([jnp.where(top_rows, pair, zero), jnp.where(top_rows, zero, pair)], 1)
        for t, (i, place, block, usable) in enumerate(slots):
            forward(2 * c + i, place, block, t + SLOTS * half, usable)

        def of(i, here, other):
            if isinstance(i, int):
                return here if i == 0 else other
            return jnp.where(i == 0, here, other)

        tops = [jnp.full((8, BLK), NEG, f32)] * 2
        for t, (i, _, _, _) in enumerate(slots):
            m = m_s[t + SLOTS * half]
            tops = [jnp.maximum(tops[0], of(i, m, NEG)), jnp.maximum(tops[1], of(i, NEG, m))]
        tops = [jnp.broadcast_to(jnp.max(top, axis=0, keepdims=True), (8, BLK)) for top in tops]
        sums, deltas = [jnp.zeros((8, BLK), f32)] * 2, [jnp.zeros((8, BLK), f32)] * 2
        for t, (i, _, _, _) in enumerate(slots):
            part = jnp.exp2((m_s[t + SLOTS * half] - of(i, tops[0], tops[1])) * factor)
            f_s[t + SLOTS * half] = part
            mass, pull = l_s[t + SLOTS * half] * part, a_s[t + SLOTS * half] * part
            sums = [sums[0] + of(i, mass, 0.0), sums[1] + of(i, 0.0, mass)]
            deltas = [deltas[0] + of(i, pull, 0.0), deltas[1] + of(i, 0.0, pull)]
        inverses = [1.0 / jnp.sum(total, axis=0, keepdims=True) for total in sums]
        deltas = [
            jnp.broadcast_to(jnp.sum(pull, axis=0, keepdims=True) * inverse, (8, BLK))
            for pull, inverse in zip(deltas, inverses)
        ]
        inverses = [jnp.broadcast_to(inverse, (8, BLK)) for inverse in inverses]
        for t, (i, _, _, _) in enumerate(slots):
            f_s[t + SLOTS * half] = f_s[t + SLOTS * half] * of(i, inverses[0], inverses[1])
            d_s[t + SLOTS * half] = of(i, deltas[0], deltas[1])

        totals = [jnp.zeros((HD, BLK), f32), jnp.zeros((HD, BLK), f32)]
        for t, (i, place, block, _) in enumerate(slots):
            term = backward(c, place, block, t, half)
            if t < WINDOW:
                totals[i] = totals[i] + term
            else:
                totals[0] = totals[0] + jnp.where(i == 0, term, 0.0)
                totals[1] = totals[1] + jnp.where(i == 0, 0.0, term)
        send_dq[c] = (jnp.concatenate(totals, 0) * SCALE).astype(bf16)
        for way in range(2):
            term = turned_dot(both[2 * c + way], pairs[c, 6 * way + 2])
            halo_out[way, c] = (term * scale_rows).astype(bf16)
        globe_acc[...] += turned_dot(both[2 * c], pairs[c, 5]) + turned_dot(both[2 * c + 1], pairs[c, 11])

    def patch_here(step):
        scattered(1, send_qo, query, step).wait_recv()
        halo_landed(shifted(col, step, -1))

        @pl.when(step + AHEAD < COLS)
        def _():
            scatter(1, send_qo, query, step + AHEAD).start()

    def patch_away(step):
        source = shifted(col, step, -1)
        to_col(2, send_dq.at[source], got_dq.at[col], step, -1).start()
        for way in range(2):
            halo_back(way, source).start()

    halo_landed(col)
    patch(col)
    own_dq = pltpu.make_async_copy(send_dq.at[col], got_dq.at[col], own_sem.at[3])
    own_dq.start()
    for way in range(2):
        halo_back(way, col).start()

    def two_patches(k):
        patch_here(2 * k + 1)
        patch_here(2 * k + 2)
        patch(shifted(col, 2 * k + 1, -1), 0)
        patch(shifted(col, 2 * k + 2, -1), 1)
        patch_away(2 * k + 1)
        patch_away(2 * k + 2)

    loop(0, COLS // 2 - 1, two_patches)
    patch_here(COLS - 1)
    patch(shifted(col, COLS - 1, -1))
    patch_away(COLS - 1)
    globe_acc[...] = globe_acc[...] * scale_rows

    @pl.when(row == 0)
    def _():
        loop(1, ROWS, lambda target: globe(target).wait_send())

    @pl.when(row != 0)
    def _():
        globe_back(row).start()

    def terms_of(q):
        left = jnp.maximum(q - 1, 0)
        right = jnp.minimum(q + 1, COLS - 1)
        sides = []
        for j in range(2):
            before = pairs[left, 6 * j + 4]
            after = pairs[right, 6 * j + 3]
            none = jnp.zeros_like(before)
            near = (
                turned_dot(both[2 * q + j], pairs[q, 6 * j])
                + turned_dot(both[2 * q + 1 - j], pairs[q, 6 * (1 - j) + 1])
                + turned_dot(both[2 * left + j], jnp.where(q > 0, before, none))
                + turned_dot(both[2 * right + j], jnp.where(q < COLS - 1, after, none))
            )
            sides.append(near)
        for c in range(COLS):
            term = pairs[c, WINDOW + q]
            term = turned_dot(both[2 * c + link_query[row, c, q]], term)
            first = link_key[row, c, q] == 0
            sides[0] = sides[0] + jnp.where(first, term, 0.0)
            sides[1] = sides[1] + jnp.where(first, 0.0, term)
        for j in range(2):
            halo_back(1 - j, q).wait_recv()
            own = sides[j] * scale_rows + halo_in[j, q].astype(f32)
            if j == 0:
                own = own + jnp.where((q == 0) & (row == 0), globe_acc[...], 0.0)
            send_terms[q, j] = own.astype(bf16)

    def send_back(step):
        q = shifted(col, step, 1)
        late = (row == 0) & (q == 0)
        terms_of(jnp.where(late, col, q))

        @pl.when(jnp.logical_not(late))
        def _():
            gather(3, send_terms, got_kv, step).start()

    loop(1, COLS, send_back)

    @pl.when(row == 0)
    def _():
        loop(1, ROWS, lambda slot: globe_back(slot).wait_recv())
        total = globe_acc[...]
        for slot in range(1, ROWS):
            total = total + globe_in[slot]
        globe_acc[...] = total

    terms_of(jnp.where(row == 0, 0, col))

    def send_late(step):
        @pl.when((row == 0) & (shifted(col, step, 1) == 0))
        def _():
            gather(3, send_terms, got_kv, step).start()

    loop(1, COLS, send_late)
    own_back = pltpu.make_async_copy(send_terms.at[col], got_kv.at[col], own_sem.at[4])
    own_back.start()

    own_dq.wait()
    own_back.wait()

    def last(step):
        to_col(2, send_dq.at[col], got_dq.at[shifted(col, step, 1)], step, 1).wait_recv()
        gathered(3, send_terms, got_kv, step).wait_recv()
        for way in range(2):
            scatter_key(way, step).wait_send()
        scatter(1, send_qo, query, step).wait_send()
        to_col(2, send_dq.at[shifted(col, step, -1)], got_dq.at[col], step, -1).wait_send()
        gather(3, send_terms, got_kv, step).wait_send()

    loop(1, COLS, last)

    def last_halo(c):
        for way in range(2):
            halo(way, c).wait_send()
            halo_back(way, c).wait_send()

    loop(0, COLS, last_halo)

    @pl.when(row != 0)
    def _():
        globe_back(row).wait_send()


def unpack(got_dq, got_kv, gq_out, gk_out, gv_out, dq, kv, wide, turned, in_sem, out_sem):
    loads = [pltpu.make_async_copy(got_dq, dq, in_sem.at[0])]
    loads += [pltpu.make_async_copy(got_kv.at[:, i], kv.at[i], in_sem.at[1 + i]) for i in range(2)]
    for load in loads:
        load.start()
    stores = []

    def turn(n, i, load, out):
        for h in range(HEADS):
            wide[n, h * HD : (h + 1) * HD, :] = load(h)
        for t in range(TILES):
            span = slice(t * BLK, (t + 1) * BLK)
            turned[n, :, span] = wide[n, span, :].T.astype(bf16)
        stores.append(pltpu.make_async_copy(turned.at[n], out.at[i], out_sem.at[n]))
        stores[-1].start()

    loads[0].wait()
    for i in range(2):
        turn(i, i, lambda h: dq[h].astype(f32)[i * HD : (i + 1) * HD], gq_out)
    for i in range(2):
        loads[1 + i].wait()
        turn(2 + 2 * i, i, lambda h: kv[i, h].astype(f32)[:HD], gk_out)
        turn(3 + 2 * i, i, lambda h: kv[i, h].astype(f32)[HD:], gv_out)
    for store in stores:
        store.wait()


VMEM = pl.BlockSpec(memory_space=pltpu.VMEM)
ANY = pl.BlockSpec(memory_space=pl.ANY)
SMEM = pl.BlockSpec(memory_space=pltpu.SMEM)
DMA = pltpu.SemaphoreType.DMA
LIMIT = 61 * 1024 * 1024


def shape(dims, kind):
    return jax.ShapeDtypeStruct(dims, kind)


SCRATCH = [
    pltpu.VMEM((2, BLK, D), bf16),
    pltpu.VMEM((2, BLK, D), bf16),
    pltpu.VMEM((D, BLK), f32),
    pltpu.VMEM((D, BLK), f32),
    pltpu.VMEM((HEADS, 2, PAIR, BLK), bf16),
    pltpu.VMEM((HEADS, 2, PAIR, BLK), bf16),
    pltpu.VMEM((2 * COLS, PAIR, BLK), bf16),
    pltpu.VMEM((EDGES, PAIR, BLK), bf16),
    pltpu.VMEM((2 * COLS, PAIR, BLK), bf16),
    pltpu.VMEM((2 * COLS, BLK, PAIR), bf16),
    pltpu.VMEM((EDGES, BLK, PAIR), bf16),
    pltpu.VMEM((2 * COLS, PAIR, 2 * BLK), bf16),
    pltpu.VMEM((COLS, SLOTS, BLK, 2 * BLK), bf16),
    pltpu.VMEM((2 * SLOTS,) + GROUPS, f32),
    pltpu.VMEM((2 * SLOTS,) + GROUPS, f32),
    pltpu.VMEM((2 * SLOTS, 8, BLK), f32),
    pltpu.VMEM((2 * SLOTS, 8, BLK), f32),
    pltpu.VMEM((2 * SLOTS, 8, BLK), f32),
    pltpu.VMEM((2 * SLOTS, 8, BLK), f32),
    pltpu.VMEM((2 * SLOTS, 8, BLK), f32),
    pltpu.VMEM((COLS, PAIR, BLK), bf16),
    pltpu.VMEM((COLS, 2, PAIR, BLK), bf16),
    pltpu.VMEM((2, COLS, PAIR, BLK), bf16),
    pltpu.VMEM((2, COLS, PAIR, BLK), bf16),
    pltpu.VMEM((PAIR, BLK), f32),
    pltpu.VMEM((ROWS, PAIR, BLK), f32),
    DMA((4,)),
    DMA((5,)),
    DMA((5, COLS)),
    DMA((5, COLS)),
    DMA((2, COLS)),
    DMA((2, COLS)),
    DMA((2, COLS)),
    DMA((2, COLS)),
    DMA((ROWS,)),
    DMA((ROWS,)),
]


def shards(queries, keys, values, dout, link_query, link_key):
    flat = [a.reshape(2, BLK, D) for a in (queries, keys, values, dout)]
    got_dq, got_kv = pl.pallas_call(
        attend,
        out_shape=(shape((HEADS, PAIR, BLK), bf16), shape((HEADS, 2, PAIR, BLK), bf16)),
        in_specs=[SMEM, SMEM] + [ANY] * 4,
        out_specs=(ANY, ANY),
        scratch_shapes=SCRATCH,
        compiler_params=pltpu.CompilerParams(collective_id=0, has_side_effects=True, vmem_limit_bytes=LIMIT),
        name="attend",
    )(link_query, link_key, *flat)
    outs = pl.pallas_call(
        unpack,
        out_shape=(shape((2, BLK, D), bf16),) * 3,
        in_specs=[ANY] * 2,
        out_specs=(ANY,) * 3,
        scratch_shapes=[
            pltpu.VMEM((HEADS, PAIR, BLK), bf16),
            pltpu.VMEM((2, HEADS, PAIR, BLK), bf16),
            pltpu.VMEM((6, D, BLK), f32),
            pltpu.VMEM((6, BLK, D), bf16),
            DMA((3,)),
            DMA((6,)),
        ],
        compiler_params=pltpu.CompilerParams(vmem_limit_bytes=LIMIT),
        name="unpack",
    )(got_dq, got_kv)
    return tuple(o.reshape(2, 1, BLK, D) for o in outs)


def solution(mesh):
    tiled = P("row", "col", None, None)
    return jax.shard_map(
        shards,
        mesh=mesh,
        in_specs=(tiled,) * 4 + (P(), P()),
        out_specs=(tiled,) * 3,
        check_vma=False,
    )
```
